256 devices in a mesh: row: 16 (over x, y), col: 16 (over z, core).
Axes of the slice: x: 4, y: 4, z: 8, core: 2. Of those that a mesh axis runs over, the one named last changes fastest.
Arguments:
- factor: float32 [4, 2048, 4, 2048], P(None, 'row', None, 'col'), may hold values from -4 to 4, as said below
- structure: int32 [4, 64], replicated, may hold values from 0 to 1, as said below
Outputs:
- inverse: float32 [4, 2048, 4, 2048], P(None, 'row', None, 'col')
The draws below stay inside these ranges and needn't reach their ends.
Inputs may be any that keep to these rules, and one draw needn't show every extreme that they name: structure[s, t] is 1 only for tiles t of proper ancestors of supernode s; row 3 is zero; where structure[0, t] or structure[1, t] is 1 for a tile t of supernode 3, structure[2, t] is 1 too. `factor`: the diagonal supernode blocks of F are symmetric.
All inputs are finite; a program needn't handle non-finite values.
Results may differ from the reference program's by a relative error of at most 0.000055.
Values sent between devices are 32-bit elements; how exact they have to be, the bound alone decides.
No kernel may reach another device: no remote copies, remote signals or barrier semaphores. Data moves between devices by JAX's collectives and lax.ppermute only.
A program may use at most 64 MiB of HBM per device.

```python
import math
import jax
import jax.numpy as jnp
from jax import lax

W = 2048
TB = 128
KR = 4
KC = 4
N_ROW = 16
N_COL = 16


def draw_factor(key, part):
    key = jax.random.fold_in(key, 11)
    first, second = jax.random.split(key, 2)
    size = 4 * W
    base = jax.random.normal(first, (size, size), jnp.float32)
    diagonal = jnp.exp(jax.random.uniform(second, (size,), jnp.float32, math.log(0.5), math.log(2.0)))
    index = jnp.arange(size)
    same_cell = index[:, None] == index[None, :]
    symmetric = (base + base.T) * (0.35 / math.sqrt(2.0 * W)) + jnp.where(same_cell, diagonal[:, None], 0.0)
    same_node = index[:, None] // W == index[None, :] // W
    matrix = jnp.where(same_node, symmetric, base * (0.9 / math.sqrt(W)))
    return matrix.reshape(KR, N_ROW * TB, KC, N_COL * TB)


def draw_structure(key, part):
    key = jax.random.fold_in(key, 23)
    tiles_each = W // TB
    bits = jax.random.randint(key, (4, 4 * tiles_each), 0, 2)
    tile_node = jnp.arange(4 * tiles_each) // tiles_each
    parent_row = bits[2] * (tile_node == 3)
    allowed = (tile_node == 2) | (tile_node == 3) & (parent_row == 1)
    child_rows = bits[0:2] * allowed[None, :]
    zero_row = jnp.zeros_like(parent_row)
    return jnp.concatenate([child_rows, parent_row[None, :], zero_row[None, :]], axis=0).astype(jnp.int32)


def setup_inputs(seed: int = 0) -> dict:
    seeds = jax.random.split(jax.random.key(seed), 3)
    factor = draw_factor(jax.random.fold_in(seeds[2], 71), 0)
    structure = draw_structure(jax.random.fold_in(seeds[2], 71), 0)
    return {"factor": factor, "structure": structure}


HIGH = lax.Precision.HIGHEST


def product(left, right):
    return jnp.dot(left, right, precision=HIGH, preferred_element_type=jnp.float32)


def block(array, row_node, col_node, row_nodes, col_nodes):
    return array[row_node * W:(row_node + row_nodes) * W, col_node * W:(col_node + col_nodes) * W]


def reference(factor, structure):
    size = 4 * W
    matrix = factor.reshape(size, size)
    index = jnp.arange(size)
    pattern = structure.T[index // TB][:, index // W] == 1
    lower = jnp.where(pattern, matrix, 0.0)
    root = block(matrix, 3, 3, 1, 1)
    factor_one = block(lower, 3, 2, 1, 1)
    image_one = jnp.where(block(pattern, 3, 2, 1, 1), -product(root, factor_one), 0.0)
    inner_two = block(matrix, 2, 2, 1, 1) - product(factor_one.T, image_one)
    ancestors = jnp.block([[inner_two, image_one.T], [image_one, root]])
    factor_two = block(lower, 2, 0, 2, 2)
    image_two = jnp.where(block(pattern, 2, 0, 2, 2), -product(ancestors, factor_two), 0.0)
    inner_zero = block(matrix, 0, 0, 1, 1) - product(factor_two[:, :W].T, image_two[:, :W])
    inner_first = block(matrix, 1, 1, 1, 1) - product(factor_two[:, W:].T, image_two[:, W:])
    empty = jnp.zeros((W, W), matrix.dtype)
    result = jnp.block([
        [inner_zero, empty, empty, empty],
        [empty, inner_first, empty, empty],
        [image_two[:W, :W], image_two[:W, W:], inner_two, empty],
        [image_two[W:, :W], image_two[W:, W:], image_one, root],
    ])
    return result.reshape(KR, N_ROW * TB, KC, N_COL * TB)
```

```python
import jax
import jax.numpy as jnp
from jax import lax
from jax.sharding import PartitionSpec as P

N = 16
TB = 128
HIGH = lax.Precision.HIGH
PAIR_SWAP = [(i, i ^ 1) for i in range(N)]
SAME_PARITY = [[p + 2 * i for i in range(N // 2)] for p in range(2)]


def swap_rows(x):
    return lax.ppermute(x, "row", PAIR_SWAP)


def gather_layers_start(x):
    parts = [x]
    for d in range(1, N // 2):
        parts.append(lax.ppermute(x, "col", [((i + 2 * d) % N, i) for i in range(N)]))
    return parts


def gather_layers_end(parts, layer, core):
    mine = jnp.zeros((N // 2,) + parts[0].shape, parts[0].dtype)
    for d, part in enumerate(parts):
        mine = lax.dynamic_update_index_in_dim(mine, part, lax.rem(layer + d, N // 2), 0)
    other = lax.ppermute(mine, "col", PAIR_SWAP)
    even = jnp.where(core == 0, mine, other)
    odd = jnp.where(core == 0, other, mine)
    return jnp.stack([even, odd])


def by_parity(panel):
    return panel.reshape((N // 2, 2) + panel.shape[1:]).swapaxes(0, 1)


def times(left, right):
    return jnp.einsum("pkmab,pkbc->mac", left, right, precision=HIGH)


def spread(left, right):
    out = jnp.einsum("pkmab,mac->kpcb", left, right, precision=HIGH)
    return out.reshape(N, TB, TB)


def body(factor, structure):
    row = lax.axis_index("row")
    col = lax.axis_index("col")
    side = lax.rem(row, 2)
    layer = col // 2
    core = lax.rem(col, 2)

    def pair(own, other):
        return jnp.where(side == 0, jnp.stack([own, other]), jnp.stack([other, own]))

    def pick(zero, one):
        return jnp.where(side == 0, zero, one)

    mask = structure.reshape(4, 4, N)
    mask = lax.dynamic_index_in_dim(mask, row, axis=2, keepdims=False) == 1

    def block(r, c):
        return factor[r, :, c, :]

    def lower(r, c):
        return jnp.where(mask[c, r], block(r, c), 0.0)

    root = block(3, 3)
    lower_32 = lower(3, 2)
    lower_2 = [lower(2, 0), lower(2, 1)]
    lower_3 = [lower(3, 0), lower(3, 1)]
    diag_2 = block(2, 2)

    with jax.named_scope("swap_first"):
        lower_32_pair = pair(lower_32, swap_rows(lower_32))
    with jax.named_scope("gather_l32"):
        parts_32 = gather_layers_start(lower_32_pair)
    with jax.named_scope("gather_l2"):
        send = jnp.broadcast_to(jnp.stack(lower_2)[None], (N // 2, 2, TB, TB)).reshape(N, TB, TB)
        l2_cols = by_parity(lax.all_to_all(send, "row", 0, 0, tiled=True))
    with jax.named_scope("swap_rest"):
        rest = jnp.stack([root, diag_2, pick(lower_2[1], lower_2[0]), pick(lower_3[1], lower_3[0])])
        other = swap_rows(rest)
    l2_pair = pair(pick(lower_2[0], lower_2[1]), other[2])
    l3_pair = pair(pick(lower_3[0], lower_3[1]), other[3])
    with jax.named_scope("sc_rows"):
        packed = jnp.concatenate([pair(root, other[0]), pair(diag_2, other[1]), l2_pair])
        panels = by_parity(lax.all_gather(packed, "col", axis=0))
        root_rows, diag_rows, l2_rows = panels[:, :, 0:2], panels[:, :, 2:4], panels[:, :, 4:6]
    with jax.named_scope("sc_l32_cols"):
        l32_cols = by_parity(lax.all_gather(lower_32, "row", axis=0))
    with jax.named_scope("gather_l32"):
        l32_rows = gather_layers_end(parts_32, layer, core)
    with jax.named_scope("term_t"):
        t_pair = times(l32_rows, l2_cols) - l3_pair
    with jax.named_scope("gather_t_rows"):
        parts_t = gather_layers_start(t_pair)
    with jax.named_scope("gather_t_cols"):
        send = jnp.broadcast_to(t_pair[None], (N // 2, 2, TB, TB))
        t_cols = lax.all_to_all(send, "row", 0, 0, tiled=True, axis_index_groups=SAME_PARITY)
        t_cols = t_cols.swapaxes(0, 1)
    with jax.named_scope("term_y"):
        y_pair = times(root_rows, t_cols)
    with jax.named_scope("term_u"):
        u_pair = times(diag_rows, l2_cols)
    with jax.named_scope("term_q"):
        root_own = lax.dynamic_index_in_dim(root_rows, side, axis=2)
        l32_own = lax.dynamic_index_in_dim(l32_rows, side, axis=2)
        q = times(root_own, l32_cols)
    with jax.named_scope("gather_t_rows"):
        t_rows = gather_layers_end(parts_t, layer, core)
    with jax.named_scope("swap_y"):
        y_away = swap_rows(pick(y_pair[1], y_pair[0]))
        y_home = pick(y_pair[0], y_pair[1])
    with jax.named_scope("sums"):
        start = row - side
        x_sum = spread(l32_rows, y_pair)
        x_sum = lax.dynamic_update_slice_in_dim(
            x_sum,
            lax.dynamic_slice_in_dim(x_sum, start, 2, 0) + u_pair.swapaxes(1, 2),
            start,
            0,
        )
        z_sum = spread(
            jnp.concatenate([t_rows, l2_rows], axis=2), jnp.concatenate([y_pair, u_pair])
        )
        q_sum = spread(l32_own, q)
        send = jnp.stack([x_sum, z_sum, q_sum], axis=1)
    with jax.named_scope("scatter_sums"):
        got = lax.all_to_all(send, "row", 0, 0, tiled=True)
    with jax.named_scope("finish"):
        both = got[:, :2].reshape(N // 2, 2, 2, TB, TB).sum(axis=0)
        x_two = -both[:, 0].swapaxes(1, 2)
        inner = both[:, 1].swapaxes(1, 2)
        inner_two = diag_2 + got[:, 2].sum(axis=0).T
        y_zero = pick(y_home, y_away)
        y_one = pick(y_away, y_home)
        empty = jnp.zeros((TB, TB), factor.dtype)

        def masked(s, r, x):
            return jnp.where(mask[s, r], x, 0.0)

        tiles = [
            [block(0, 0) + inner[0], empty, empty, empty],
            [empty, block(1, 1) + inner[1], empty, empty],
            [masked(0, 2, x_two[0]), masked(1, 2, x_two[1]), inner_two, empty],
            [masked(0, 3, y_zero), masked(1, 3, y_one), masked(2, 3, -q[0]), root],
        ]
        return jnp.stack([jnp.stack(t, axis=1) for t in tiles])


def solution(mesh):
    return jax.shard_map(
        body,
        mesh=mesh,
        in_specs=(P(None, "row", None, "col"), P()),
        out_specs=P(None, "row", None, "col"),
        check_vma=False,
    )
```

```python
import jax
import jax.numpy as jnp
from jax import lax
from jax.experimental import pallas as pl
from jax.experimental.pallas import tpu as pltpu
from jax.sharding import PartitionSpec as P

N = 16
LAYERS = 8
TB = 128
F32 = jnp.float32
BF16 = jnp.bfloat16
CORE_SWAP = [(i, i ^ 1) for i in range(N)]
LAYER_UP = [(i, (i + 2) % N) for i in range(N)]
LAYER_DOWN = [(i, (i - 2) % N) for i in range(N)]


def split(x):
    high = x.astype(BF16)
    return high, (x - high.astype(F32)).astype(BF16)


def dot3(a, b):
    a_high, a_low = a
    b_high, b_low = b

    def one(x, y):
        return jnp.dot(x, y, preferred_element_type=F32)

    return one(a_high, b_high) + (one(a_high, b_low) + one(a_low, b_high))


def lanes(*tiles):
    return jnp.concatenate(tiles, axis=1)


def rows(*tiles):
    return jnp.concatenate(tiles, axis=0)


def tile(r, c):
    return pl.ds(r * 4 * TB + c, TB, stride=4)


def call(kernel, shapes, *args, scalars=1):
    smem = pl.BlockSpec(memory_space=pltpu.SMEM)
    vmem = pl.BlockSpec(memory_space=pltpu.VMEM)
    return pl.pallas_call(
        kernel,
        out_shape=[jax.ShapeDtypeStruct(s, F32) for s in shapes],
        in_specs=[smem] * scalars + [vmem] * (len(args) - scalars),
        out_specs=[vmem] * len(shapes),
        compiler_params=pltpu.CompilerParams(vmem_limit_bytes=28 * 2**20),
    )(*args)


def prepare_kernel(mask_ref, f_ref, l32_ref, packed_ref, send_ref, l3_ref):
    def lower(r, c):
        return jnp.where(mask_ref[c, r] == 1, f_ref[tile(r, c), :], 0.0)

    l32_ref[0] = lower(3, 2)
    packed_ref[0] = f_ref[tile(3, 3), :]
    packed_ref[1] = f_ref[tile(2, 2), :]
    for s in range(2):
        x = lower(2, s)
        packed_ref[2 + s] = x
        for k in range(N):
            send_ref[k, s] = x
        l3_ref[s] = lower(3, s)


def places(place_ref, d):
    layer, core = place_ref[0] // 2, lax.rem(place_ref[0], 2)
    k = lax.rem(layer + d, LAYERS) * 2
    return k + core, k + 1 - core


def t_kernel(place_ref, mine_ref, other_ref, l2_ref, l3_ref, t_ref, send_ref):
    total = jnp.zeros((TB, 2 * TB), F32)
    for d in range(LAYERS):
        k0, k1 = places(place_ref, d)
        a = split(lanes(mine_ref[d, 0], other_ref[d, 0]))
        b = split(rows(lanes(l2_ref[k0, 0], l2_ref[k0, 1]), lanes(l2_ref[k1, 0], l2_ref[k1, 1])))
        total += dot3(a, b)
    for s in range(2):
        x = total[:, s * TB : (s + 1) * TB] - l3_ref[s]
        t_ref[s] = x
        for k in range(N):
            send_ref[k, s] = x


def uq_kernel(rows_ref, l2_ref, l32_ref, u_ref, q_ref):
    u = jnp.zeros((TB, 2 * TB), F32)
    q = jnp.zeros((TB, TB), F32)
    for k in range(0, N, 2):
        b = split(rows(lanes(l2_ref[k, 0], l2_ref[k, 1]), lanes(l2_ref[k + 1, 0], l2_ref[k + 1, 1])))
        u += dot3(split(lanes(rows_ref[k, 1], rows_ref[k + 1, 1])), b)
        b = split(rows(l32_ref[k], l32_ref[k + 1]))
        q += dot3(split(lanes(rows_ref[k, 0], rows_ref[k + 1, 0])), b)
    for s in range(2):
        u_ref[s] = u[:, s * TB : (s + 1) * TB]
    q_ref[...] = q


def y_kernel(rows_ref, t_ref, y_ref):
    y = jnp.zeros((TB, 2 * TB), F32)
    for k in range(0, N, 2):
        b = split(rows(lanes(t_ref[k, 0], t_ref[k, 1]), lanes(t_ref[k + 1, 0], t_ref[k + 1, 1])))
        y += dot3(split(lanes(rows_ref[k, 0], rows_ref[k + 1, 0])), b)
    for s in range(2):
        y_ref[s] = y[:, s * TB : (s + 1) * TB]


def sums_kernel(
    place_ref, y_ref, u_ref, q_ref, l_mine_ref, l_other_ref, t_mine_ref, t_other_ref, rows_ref, sum_ref
):
    row = place_ref[1]
    y = [y_ref[s].T for s in range(2)]
    u = [u_ref[s].T for s in range(2)]
    left = split(rows(y[0], y[1], q_ref[...].T))
    pair = [split(lanes(y[s], u[s])) for s in range(2)]
    for d in range(LAYERS):
        ks = places(place_ref, d)
        x = dot3(left, split(lanes(l_mine_ref[d, 0], l_other_ref[d, 0])))
        for i, k in enumerate(ks):
            part = x[:, i * TB : (i + 1) * TB]
            sum_ref[k, 0] = part[:TB]
            sum_ref[k, 1] = part[TB : 2 * TB]
            sum_ref[k, 4] = part[2 * TB :]
        for s in range(2):
            b = rows(
                lanes(t_mine_ref[d, s], t_other_ref[d, s]),
                lanes(rows_ref[ks[0], 2 + s], rows_ref[ks[1], 2 + s]),
            )
            z = dot3(pair[s], split(b))
            for i, k in enumerate(ks):
                sum_ref[k, 2 + s] = z[:, i * TB : (i + 1) * TB]
    for s in range(2):
        sum_ref[row, s] += u[s]


def finish_kernel(mask_ref, f_ref, got_ref, y_ref, q_ref, out_ref):
    def total(i):
        x = got_ref[0, i]
        for k in range(1, N):
            x += got_ref[k, i]
        return x.T

    def masked(s, r, x):
        return jnp.where(mask_ref[s, r] == 1, x, 0.0)

    empty = jnp.zeros((TB, TB), F32)
    for r, c in ((0, 1), (0, 2), (0, 3), (1, 0), (1, 2), (1, 3), (2, 3)):
        out_ref[tile(r, c), :] = empty
    for s in range(2):
        out_ref[tile(s, s), :] = f_ref[tile(s, s), :] + total(2 + s)
        out_ref[tile(2, s), :] = masked(s, 2, -total(s))
        out_ref[tile(3, s), :] = masked(s, 3, y_ref[s])
    out_ref[tile(2, 2), :] = f_ref[tile(2, 2), :] + total(4)
    out_ref[tile(3, 2), :] = masked(2, 3, -q_ref[...])
    out_ref[tile(3, 3), :] = f_ref[tile(3, 3), :]


def gather_layers(x):
    found = {0: x}
    up = down = x
    for step in range(1, LAYERS // 2):
        up = lax.ppermute(up, "col", LAYER_UP)
        down = lax.ppermute(down, "col", LAYER_DOWN)
        found[LAYERS - step] = up
        found[step] = down
    half = TB // 2
    found[LAYERS // 2] = jnp.concatenate(
        [
            lax.ppermute(up[:, :half], "col", LAYER_UP),
            lax.ppermute(down[:, half:], "col", LAYER_DOWN),
        ],
        axis=1,
    )
    mine = jnp.stack([found[d] for d in range(LAYERS)])
    return mine, lax.ppermute(mine, "col", CORE_SWAP)


def body(factor, structure):
    row = lax.axis_index("row")
    col = lax.axis_index("col")
    place = jnp.stack([col, row]).astype(jnp.int32)
    mask = structure.reshape(4, 4, N)
    mask = lax.dynamic_index_in_dim(mask, row, axis=2, keepdims=False)
    flat = factor.reshape(N * TB, TB)
    square = (TB, TB)

    with jax.named_scope("prepare"):
        l32, packed, send, l3 = call(
            prepare_kernel, [(1, *square), (4, *square), (N, 2, *square), (2, *square)], mask, flat
        )
    with jax.named_scope("gather_l2_cols"):
        l2_cols = lax.all_to_all(send, "row", 0, 0, tiled=True)
    with jax.named_scope("gather_l32_rows"):
        l_mine, l_other = gather_layers(l32)
    with jax.named_scope("gather_rows"):
        panels = lax.all_gather(packed, "col", axis=0)
    with jax.named_scope("gather_l32_cols"):
        l32_cols = lax.all_gather(l32[0], "row", axis=0)
    with jax.named_scope("term_t"):
        t, send = call(
            t_kernel, [(2, *square), (N, 2, *square)], place, l_mine, l_other, l2_cols, l3
        )
    with jax.named_scope("gather_t_cols"):
        t_cols = lax.all_to_all(send, "row", 0, 0, tiled=True)
    with jax.named_scope("gather_t_rows"):
        t_mine, t_other = gather_layers(t)
    with jax.named_scope("term_uq"):
        u, q = call(uq_kernel, [(2, *square), square], panels, l2_cols, l32_cols, scalars=0)
    with jax.named_scope("term_y"):
        (y,) = call(y_kernel, [(2, *square)], panels, t_cols, scalars=0)
    with jax.named_scope("sums"):
        (sums,) = call(
            sums_kernel,
            [(N, 5, *square)],
            place,
            y,
            u,
            q,
            l_mine,
            l_other,
            t_mine,
            t_other,
            panels,
        )
    with jax.named_scope("scatter_sums"):
        got = lax.all_to_all(sums, "row", 0, 0, tiled=True)
    with jax.named_scope("finish"):
        (out,) = call(finish_kernel, [(N * TB, TB)], mask, flat, got, y, q)
        return out.reshape(factor.shape)


def solution(mesh):
    return jax.shard_map(
        body,
        mesh=mesh,
        in_specs=(P(None, "row", None, "col"), P()),
        out_specs=P(None, "row", None, "col"),
        check_vma=False,
    )
```

```python
import jax
import jax.numpy as jnp
from jax import lax
from jax.experimental import pallas as pl
from jax.experimental.pallas import tpu as pltpu
from jax.sharding import PartitionSpec as P

N = 16
LAYERS = 8
TB = 128
F32 = jnp.float32
BF16 = jnp.bfloat16
CORE_SWAP = [(i, i ^ 1) for i in range(N)]
ROW_SWAP = [(i, i ^ 1) for i in range(N)]
SAME_SIDE = [[p + 2 * i for i in range(N // 2)] for p in range(2)]
LAYER_UP = [(i, (i + 2) % N) for i in range(N)]
LAYER_DOWN = [(i, (i - 2) % N) for i in range(N)]


def split(x):
    high = x.astype(BF16)
    return high, (x - high.astype(F32)).astype(BF16)


def dot3(a, b):
    a_high, a_low = a
    b_high, b_low = b

    def one(x, y):
        return jnp.dot(x, y, preferred_element_type=F32)

    return one(a_high, b_high) + (one(a_high, b_low) + one(a_low, b_high))


def lanes(*tiles):
    return jnp.concatenate(tiles, axis=1)


def rows(*tiles):
    return jnp.concatenate(tiles, axis=0)


def tile(r, c):
    return pl.ds(r * 4 * TB + c, TB, stride=4)


def call(kernel, shapes, *args, scalars=1):
    smem = pl.BlockSpec(memory_space=pltpu.SMEM)
    vmem = pl.BlockSpec(memory_space=pltpu.VMEM)
    return pl.pallas_call(
        kernel,
        out_shape=[jax.ShapeDtypeStruct(s, F32) for s in shapes],
        in_specs=[smem] * scalars + [vmem] * (len(args) - scalars),
        out_specs=[vmem] * len(shapes),
        compiler_params=pltpu.CompilerParams(vmem_limit_bytes=28 * 2**20),
    )(*args)


def prepare_kernel(mask_ref, place_ref, f_ref, l32_ref, away_ref, home_ref, send_ref):
    side = lax.rem(place_ref[1], 2)

    def lower(r, c):
        return jnp.where(mask_ref[c, r] == 1, f_ref[tile(r, c), :], 0.0)

    x = lower(3, 2)
    l32_ref[...] = x
    l2 = [lower(2, s) for s in range(2)]
    l3 = [lower(3, s) for s in range(2)]
    for k in range(N):
        send_ref[k, 0] = l2[k % 2]
        send_ref[k, 1] = x
    root, diag = f_ref[tile(3, 3), :], f_ref[tile(2, 2), :]
    away_ref[0] = home_ref[0] = root
    away_ref[1] = home_ref[1] = diag
    even = side == 0
    home_ref[2] = jnp.where(even, l2[0], l2[1])
    away_ref[2] = jnp.where(even, l2[1], l2[0])
    home_ref[3] = jnp.where(even, l3[0], l3[1])
    away_ref[3] = jnp.where(even, l3[1], l3[0])


def pack_kernel(place_ref, home_ref, got_ref, packed_ref, l3_ref):
    side = lax.rem(place_ref[1], 2)
    for i in range(3):
        packed_ref[i, side] = home_ref[i]
        packed_ref[i, 1 - side] = got_ref[i]
    l3_ref[side] = home_ref[3]
    l3_ref[1 - side] = got_ref[3]


def places(place_ref, d):
    layer, core = place_ref[0] // 2, lax.rem(place_ref[0], 2)
    k = lax.rem(layer + d, LAYERS) * 2
    return k + core, k + 1 - core


def t_kernel(place_ref, mine_ref, other_ref, l2_ref, l3_ref, t_ref, send_ref):
    total = jnp.zeros((2 * TB, TB), F32)
    for d in range(LAYERS):
        k0, k1 = places(place_ref, d)
        a = rows(*(lanes(mine_ref[d, i], other_ref[d, i]) for i in range(2)))
        total += dot3(split(a), split(rows(l2_ref[k0, 0], l2_ref[k1, 0])))
    for i in range(2):
        x = total[i * TB : (i + 1) * TB] - l3_ref[i]
        t_ref[i] = x
        for k in range(N // 2):
            send_ref[k, i] = x


def pair_rows(rows_ref, k, i):
    return rows(*(lanes(rows_ref[k, i, j], rows_ref[k + 1, i, j]) for j in range(2)))


def uq_kernel(place_ref, rows_ref, cols_ref, u_ref, q_ref):
    side = lax.rem(place_ref[1], 2)
    u = jnp.zeros((2 * TB, TB), F32)
    q = jnp.zeros((TB, TB), F32)
    for k in range(0, N, 2):
        b = split(rows(cols_ref[k, 0], cols_ref[k + 1, 0]))
        u += dot3(split(pair_rows(rows_ref, k, 1)), b)
        b = split(rows(cols_ref[k, 1], cols_ref[k + 1, 1]))
        q += dot3(split(lanes(rows_ref[k, 0, side], rows_ref[k + 1, 0, side])), b)
    for i in range(2):
        u_ref[i] = u[i * TB : (i + 1) * TB]
    q_ref[...] = q


def y_kernel(place_ref, rows_ref, t_ref, y_ref, home_ref, away_ref):
    side = lax.rem(place_ref[1], 2)
    y = jnp.zeros((2 * TB, TB), F32)
    for k in range(0, N, 2):
        b = split(rows(t_ref[k // 2, 0], t_ref[k // 2, 1]))
        y += dot3(split(pair_rows(rows_ref, k, 0)), b)
    y_ref[...] = y
    even = side == 0
    home_ref[...] = jnp.where(even, y[:TB], y[TB:])
    away_ref[...] = jnp.where(even, y[TB:], y[:TB])


def sums_kernel(
    place_ref, y_ref, u_ref, q_ref, l_mine_ref, l_other_ref, t_mine_ref, t_other_ref, rows_ref, sum_ref
):
    row = place_ref[1]
    side = lax.rem(row, 2)
    y = y_ref[...].T
    u = [u_ref[i].T for i in range(2)]
    y_split = split(y)
    yu_split = split(lanes(y, *u))
    q_split = split(q_ref[...].T)
    for d in range(LAYERS):
        ks = places(place_ref, d)
        l32 = rows(*(lanes(l_mine_ref[d, i], l_other_ref[d, i]) for i in range(2)))
        l32_own = lanes(l_mine_ref[d, side], l_other_ref[d, side])
        low = [lanes(t_mine_ref[d, i], t_other_ref[d, i]) for i in range(2)]
        low += [lanes(rows_ref[ks[0], 2, i], rows_ref[ks[1], 2, i]) for i in range(2)]
        parts = [
            dot3(y_split, split(l32)),
            dot3(yu_split, split(rows(*low))),
            dot3(q_split, split(l32_own)),
        ]
        for j, part in enumerate(parts):
            for i, k in enumerate(ks):
                sum_ref[k, j] = part[:, i * TB : (i + 1) * TB]
    for i in range(2):
        sum_ref[row - side + i, 0] += u[i]


def finish_kernel(mask_ref, place_ref, f_ref, got_ref, home_ref, away_ref, q_ref, out_ref):
    even = lax.rem(place_ref[1], 2) == 0

    def total(i, ks):
        x = got_ref[ks[0], i]
        for k in ks[1:]:
            x += got_ref[k, i]
        return x.T

    def masked(s, r, x):
        return jnp.where(mask_ref[s, r] == 1, x, 0.0)

    empty = jnp.zeros((TB, TB), F32)
    for r, c in ((0, 1), (0, 2), (0, 3), (1, 0), (1, 2), (1, 3), (2, 3)):
        out_ref[tile(r, c), :] = empty
    home, away = home_ref[...], away_ref[...]
    y = [jnp.where(even, home, away), jnp.where(even, away, home)]
    for s in range(2):
        ks = range(s, N, 2)
        out_ref[tile(s, s), :] = f_ref[tile(s, s), :] + total(1, ks)
        out_ref[tile(2, s), :] = masked(s, 2, -total(0, ks))
        out_ref[tile(3, s), :] = masked(s, 3, y[s])
    out_ref[tile(2, 2), :] = f_ref[tile(2, 2), :] + total(2, range(N))
    out_ref[tile(3, 2), :] = masked(2, 3, -q_ref[...])
    out_ref[tile(3, 3), :] = f_ref[tile(3, 3), :]


def gather_layers(x, beside=None):
    found = {0: x}
    up = down = x
    for step in range(1, LAYERS // 2):
        up = lax.ppermute(up, "col", LAYER_UP)
        down = lax.ppermute(down, "col", LAYER_DOWN)
        found[LAYERS - step] = up
        found[step] = down
    half = TB // 2
    found[LAYERS // 2] = jnp.concatenate(
        [
            lax.ppermute(up[:, :half], "col", LAYER_UP),
            lax.ppermute(down[:, half:], "col", LAYER_DOWN),
        ],
        axis=1,
    )
    mine = jnp.stack([found[d] for d in range(LAYERS)])
    mine, beside = lax.optimization_barrier((mine, beside))
    return mine, lax.ppermute(mine, "col", CORE_SWAP), beside


def body(factor, structure):
    row = lax.axis_index("row")
    col = lax.axis_index("col")
    place = jnp.stack([col, row]).astype(jnp.int32)
    mask = structure.reshape(4, 4, N)
    mask = lax.dynamic_index_in_dim(mask, row, axis=2, keepdims=False)
    flat = factor.reshape(N * TB, TB)
    square = (TB, TB)

    with jax.named_scope("prepare"):
        l32, away, home, send = call(
            prepare_kernel,
            [square, (4, *square), (4, *square), (N, 2, *square)],
            mask,
            place,
            flat,
            scalars=2,
        )
    with jax.named_scope("swap_l32"):
        l32_away = lax.ppermute(l32, "row", ROW_SWAP)
        even = lax.rem(row, 2) == 0
        l32_pair = jnp.stack([jnp.where(even, l32, l32_away), jnp.where(even, l32_away, l32)])
        l32_pair, away = lax.optimization_barrier((l32_pair, away))
    with jax.named_scope("swap_rest"):
        packed, l3 = call(
            pack_kernel,
            [(3, 2, *square), (2, *square)],
            place,
            home,
            lax.ppermute(away, "row", ROW_SWAP),
        )
    with jax.named_scope("gather_cols"):
        cols = lax.all_to_all(send, "row", 0, 0, tiled=True)
    with jax.named_scope("gather_l32_rows"):
        l_mine, l_other, cols = gather_layers(l32_pair, cols)
    with jax.named_scope("gather_rows"):
        panels = lax.all_gather(packed, "col", axis=0)
    with jax.named_scope("term_t"):
        t, send = call(
            t_kernel, [(2, *square), (N // 2, 2, *square)], place, l_mine, l_other, cols, l3
        )
    with jax.named_scope("gather_t_cols"):
        t_cols = lax.all_to_all(
            send, "row", 0, 0, tiled=True, axis_index_groups=SAME_SIDE
        )
    with jax.named_scope("gather_t_rows"):
        t_mine, t_other, t_cols = gather_layers(t, t_cols)
    with jax.named_scope("term_uq"):
        u, q = call(uq_kernel, [(2, *square), square], place, panels, cols)
    with jax.named_scope("term_y"):
        y, y_home, y_away = call(
            y_kernel, [(2 * TB, TB), square, square], place, panels, t_cols
        )
    with jax.named_scope("swap_y"):
        y_away = lax.ppermute(y_away, "row", ROW_SWAP)
    with jax.named_scope("sums"):
        (sums,) = call(
            sums_kernel,
            [(N, 3, *square)],
            place,
            y,
            u,
            q,
            l_mine,
            l_other,
            t_mine,
            t_other,
            panels,
        )
    with jax.named_scope("scatter_sums"):
        got = lax.all_to_all(sums, "row", 0, 0, tiled=True)
    with jax.named_scope("finish"):
        (out,) = call(
            finish_kernel, [(N * TB, TB)], mask, place, flat, got, y_home, y_away, q, scalars=2
        )
        return out.reshape(factor.shape)


def solution(mesh):
    return jax.shard_map(
        body,
        mesh=mesh,
        in_specs=(P(None, "row", None, "col"), P()),
        out_specs=P(None, "row", None, "col"),
        check_vma=False,
    )
```

```python
import jax
import jax.numpy as jnp
from jax import lax
from jax.experimental import pallas as pl
from jax.experimental.pallas import tpu as pltpu
from jax.sharding import PartitionSpec as P

N = 16
LAYERS = 8
TB = 128
F32 = jnp.float32
BF16 = jnp.bfloat16
CORE_SWAP = [(i, i ^ 1) for i in range(N)]
ROW_SWAP = [(i, i ^ 1) for i in range(N)]
SAME_SIDE = [[p + 2 * i for i in range(N // 2)] for p in range(2)]
LAYER_UP = [(i, (i + 2) % N) for i in range(N)]
LAYER_DOWN = [(i, (i - 2) % N) for i in range(N)]


def split(x):
    high = x.astype(BF16)
    return high, (x - high.astype(F32)).astype(BF16)


def dot3(a, b):
    a_high, a_low = a
    b_high, b_low = b

    def one(x, y):
        return jnp.dot(x, y, preferred_element_type=F32)

    return one(a_high, b_high) + (one(a_high, b_low) + one(a_low, b_high))


def lanes(*tiles):
    return jnp.concatenate(tiles, axis=1)


def rows(*tiles):
    return jnp.concatenate(tiles, axis=0)


def tile(r, c):
    return pl.ds(r * 4 * TB + c, TB, stride=4)


def call(kernel, shapes, *args, scalars=1):
    smem = pl.BlockSpec(memory_space=pltpu.SMEM)
    vmem = pl.BlockSpec(memory_space=pltpu.VMEM)
    return pl.pallas_call(
        kernel,
        out_shape=[jax.ShapeDtypeStruct(s, F32) for s in shapes],
        in_specs=[smem] * scalars + [vmem] * (len(args) - scalars),
        out_specs=[vmem] * len(shapes),
        compiler_params=pltpu.CompilerParams(vmem_limit_bytes=28 * 2**20),
    )(*args)


def prepare_kernel(mask_ref, place_ref, f_ref, l32_ref, away_ref, home_ref, send_ref):
    side = lax.rem(place_ref[1], 2)

    def lower(r, c):
        return jnp.where(mask_ref[c, r] == 1, f_ref[tile(r, c), :], 0.0)

    x = lower(3, 2)
    l32_ref[...] = x
    l2 = [lower(2, s) for s in range(2)]
    l3 = [lower(3, s) for s in range(2)]
    for k in range(N):
        send_ref[k] = l2[k % 2]
    root, diag = f_ref[tile(3, 3), :], f_ref[tile(2, 2), :]
    away_ref[0] = home_ref[0] = root
    away_ref[1] = home_ref[1] = diag
    even = side == 0
    home_ref[2] = jnp.where(even, l2[0], l2[1])
    away_ref[2] = jnp.where(even, l2[1], l2[0])
    home_ref[3] = jnp.where(even, l3[0], l3[1])
    away_ref[3] = jnp.where(even, l3[1], l3[0])


def pack_kernel(place_ref, home_ref, got_ref, packed_ref, l3_ref):
    side = lax.rem(place_ref[1], 2)
    for i in range(3):
        packed_ref[i, side] = home_ref[i]
        packed_ref[i, 1 - side] = got_ref[i]
    l3_ref[side] = home_ref[3]
    l3_ref[1 - side] = got_ref[3]


def places(place_ref, d):
    layer, core = place_ref[0] // 2, lax.rem(place_ref[0], 2)
    k = lax.rem(layer + d, LAYERS) * 2
    return k + core, k + 1 - core


def t_kernel(place_ref, mine_ref, other_ref, l2_ref, l3_ref, t_ref, send_ref):
    total = jnp.zeros((2 * TB, TB), F32)
    for d in range(LAYERS):
        k0, k1 = places(place_ref, d)
        a = rows(*(lanes(mine_ref[d, i], other_ref[d, i]) for i in range(2)))
        total += dot3(split(a), split(rows(l2_ref[k0], l2_ref[k1])))
    for i in range(2):
        x = total[i * TB : (i + 1) * TB] - l3_ref[i]
        t_ref[i] = x
        for k in range(N // 2):
            send_ref[k, i] = x


def pair_rows(rows_ref, k, i):
    return rows(*(lanes(rows_ref[k, i, j], rows_ref[k + 1, i, j]) for j in range(2)))


def uq_kernel(place_ref, rows_ref, l2_ref, l32_ref, u_ref, q_ref):
    side = lax.rem(place_ref[1], 2)
    u = jnp.zeros((2 * TB, TB), F32)
    q = jnp.zeros((TB, TB), F32)
    for k in range(0, N, 2):
        b = split(rows(l2_ref[k], l2_ref[k + 1]))
        u += dot3(split(pair_rows(rows_ref, k, 1)), b)
        b = split(rows(l32_ref[k], l32_ref[k + 1]))
        q += dot3(split(lanes(rows_ref[k, 0, side], rows_ref[k + 1, 0, side])), b)
    for i in range(2):
        u_ref[i] = u[i * TB : (i + 1) * TB]
    q_ref[...] = q


def y_kernel(place_ref, rows_ref, t_ref, y_ref, home_ref, away_ref):
    side = lax.rem(place_ref[1], 2)
    y = jnp.zeros((2 * TB, TB), F32)
    for k in range(0, N, 2):
        b = split(rows(t_ref[k // 2, 0], t_ref[k // 2, 1]))
        y += dot3(split(pair_rows(rows_ref, k, 0)), b)
    y_ref[...] = y
    even = side == 0
    home_ref[...] = jnp.where(even, y[:TB], y[TB:])
    away_ref[...] = jnp.where(even, y[TB:], y[:TB])


def sums_kernel(
    place_ref, y_ref, u_ref, q_ref, l_mine_ref, l_other_ref, t_mine_ref, t_other_ref, rows_ref, sum_ref
):
    row = place_ref[1]
    side = lax.rem(row, 2)
    y = y_ref[...].T
    u = [u_ref[i].T for i in range(2)]
    y_split = split(y)
    yu_split = split(lanes(y, *u))
    q_split = split(q_ref[...].T)
    for d in range(LAYERS):
        ks = places(place_ref, d)
        l32 = rows(*(lanes(l_mine_ref[d, i], l_other_ref[d, i]) for i in range(2)))
        l32_own = lanes(l_mine_ref[d, side], l_other_ref[d, side])
        low = [lanes(t_mine_ref[d, i], t_other_ref[d, i]) for i in range(2)]
        low += [lanes(rows_ref[ks[0], 2, i], rows_ref[ks[1], 2, i]) for i in range(2)]
        parts = [
            dot3(y_split, split(l32)),
            dot3(yu_split, split(rows(*low))),
            dot3(q_split, split(l32_own)),
        ]
        for j, part in enumerate(parts):
            for i, k in enumerate(ks):
                sum_ref[k, j] = part[:, i * TB : (i + 1) * TB]
    for i in range(2):
        sum_ref[row - side + i, 0] += u[i]


def finish_kernel(mask_ref, place_ref, f_ref, got_ref, home_ref, away_ref, q_ref, out_ref):
    even = lax.rem(place_ref[1], 2) == 0

    def total(i, ks):
        x = got_ref[ks[0], i]
        for k in ks[1:]:
            x += got_ref[k, i]
        return x.T

    def masked(s, r, x):
        return jnp.where(mask_ref[s, r] == 1, x, 0.0)

    empty = jnp.zeros((TB, TB), F32)
    for r, c in ((0, 1), (0, 2), (0, 3), (1, 0), (1, 2), (1, 3), (2, 3)):
        out_ref[tile(r, c), :] = empty
    home, away = home_ref[...], away_ref[...]
    y = [jnp.where(even, home, away), jnp.where(even, away, home)]
    for s in range(2):
        ks = range(s, N, 2)
        out_ref[tile(s, s), :] = f_ref[tile(s, s), :] + total(1, ks)
        out_ref[tile(2, s), :] = masked(s, 2, -total(0, ks))
        out_ref[tile(3, s), :] = masked(s, 3, y[s])
    out_ref[tile(2, 2), :] = f_ref[tile(2, 2), :] + total(2, range(N))
    out_ref[tile(3, 2), :] = masked(2, 3, -q_ref[...])
    out_ref[tile(3, 3), :] = f_ref[tile(3, 3), :]


def gather_layers(x, ties):
    found = {0: x}
    up = down = x
    tied = []
    for step in range(1, LAYERS // 2):
        up = lax.ppermute(up, "col", LAYER_UP)
        down = lax.ppermute(down, "col", LAYER_DOWN)
        if step in ties:
            up, down, other = lax.optimization_barrier((up, down, ties[step]))
            tied.append(other)
        found[LAYERS - step] = up
        found[step] = down
    half = TB // 2
    found[LAYERS // 2] = jnp.concatenate(
        [
            lax.ppermute(up[:, :half], "col", LAYER_UP),
            lax.ppermute(down[:, half:], "col", LAYER_DOWN),
        ],
        axis=1,
    )
    mine = jnp.stack([found[d] for d in range(LAYERS)])
    if LAYERS // 2 in ties:
        mine, other = lax.optimization_barrier((mine, ties[LAYERS // 2]))
        tied.append(other)
    return (mine, lax.ppermute(mine, "col", CORE_SWAP), *tied)


def body(factor, structure):
    row = lax.axis_index("row")
    col = lax.axis_index("col")
    place = jnp.stack([col, row]).astype(jnp.int32)
    mask = structure.reshape(4, 4, N)
    mask = lax.dynamic_index_in_dim(mask, row, axis=2, keepdims=False)
    flat = factor.reshape(N * TB, TB)
    square = (TB, TB)

    with jax.named_scope("prepare"):
        l32, away, home, send = call(
            prepare_kernel,
            [square, (4, *square), (4, *square), (N, *square)],
            mask,
            place,
            flat,
            scalars=2,
        )
    with jax.named_scope("swap_l32"):
        l32_away = lax.ppermute(l32, "row", ROW_SWAP)
        even = lax.rem(row, 2) == 0
        l32_pair = jnp.stack([jnp.where(even, l32, l32_away), jnp.where(even, l32_away, l32)])
    with jax.named_scope("gather_l2_cols"):
        l2_cols = lax.all_to_all(send, "row", 0, 0, tiled=True)
    with jax.named_scope("gather_l32_cols"):
        send = jnp.broadcast_to(l32[None], (N, *square))
        l32_cols = lax.all_to_all(send, "row", 0, 0, tiled=True)
    with jax.named_scope("swap_rest"):
        away = lax.ppermute(away, "row", ROW_SWAP)
    with jax.named_scope("gather_l32_rows"):
        l_mine, l_other, (away, l2_cols), l32_cols = gather_layers(
            l32_pair, {2: (away, l2_cols), 4: l32_cols}
        )
    with jax.named_scope("pack"):
        packed, l3 = call(pack_kernel, [(3, 2, *square), (2, *square)], place, home, away)
    with jax.named_scope("gather_rows"):
        panels = lax.all_gather(packed, "col", axis=0)
    with jax.named_scope("term_t"):
        t, send = call(
            t_kernel, [(2, *square), (N // 2, 2, *square)], place, l_mine, l_other, l2_cols, l3
        )
    with jax.named_scope("gather_t_cols"):
        t_cols = lax.all_to_all(
            send, "row", 0, 0, tiled=True, axis_index_groups=SAME_SIDE
        )
    with jax.named_scope("gather_t_rows"):
        t_mine, t_other, t_cols = gather_layers(t, {3: t_cols})
    with jax.named_scope("term_uq"):
        u, q = call(uq_kernel, [(2, *square), square], place, panels, l2_cols, l32_cols)
    with jax.named_scope("term_y"):
        y, y_home, y_away = call(
            y_kernel, [(2 * TB, TB), square, square], place, panels, t_cols
        )
    with jax.named_scope("swap_y"):
        y_away = lax.ppermute(y_away, "row", ROW_SWAP)
    with jax.named_scope("sums"):
        (sums,) = call(
            sums_kernel,
            [(N, 3, *square)],
            place,
            y,
            u,
            q,
            l_mine,
            l_other,
            t_mine,
            t_other,
            panels,
        )
    with jax.named_scope("scatter_sums"):
        sums, y_away = lax.optimization_barrier((sums, y_away))
        got = lax.all_to_all(sums, "row", 0, 0, tiled=True)
    with jax.named_scope("finish"):
        (out,) = call(
            finish_kernel, [(N * TB, TB)], mask, place, flat, got, y_home, y_away, q, scalars=2
        )
        return out.reshape(factor.shape)


def solution(mesh):
    return jax.shard_map(
        body,
        mesh=mesh,
        in_specs=(P(None, "row", None, "col"), P()),
        out_specs=P(None, "row", None, "col"),
        check_vma=False,
    )
```

```python
import jax
import jax.numpy as jnp
from jax import lax
from jax.experimental import pallas as pl
from jax.experimental.pallas import tpu as pltpu
from jax.sharding import PartitionSpec as P

N = 16
LAYERS = 8
TB = 128
F32 = jnp.float32
BF16 = jnp.bfloat16
CORE_SWAP = [(i, i ^ 1) for i in range(N)]
ROW_SWAP = [(i, i ^ 1) for i in range(N)]
SAME_SIDE = [[p + 2 * i for i in range(N // 2)] for p in range(2)]
LAYER_UP = [(i, (i + 2) % N) for i in range(N)]
LAYER_DOWN = [(i, (i - 2) % N) for i in range(N)]


def split(x):
    high = x.astype(BF16)
    return high, (x - high.astype(F32)).astype(BF16)


def dot3(a, b):
    a_high, a_low = a
    b_high, b_low = b

    def one(x, y):
        return jnp.dot(x, y, preferred_element_type=F32)

    return one(a_high, b_high) + (one(a_high, b_low) + one(a_low, b_high))


def lanes(*tiles):
    return jnp.concatenate(tiles, axis=1)


def rows(*tiles):
    return jnp.concatenate(tiles, axis=0)


def tile(r, c):
    return pl.ds(r * 4 * TB + c, TB, stride=4)


def call(kernel, shapes, *args, scalars=1):
    smem = pl.BlockSpec(memory_space=pltpu.SMEM)
    vmem = pl.BlockSpec(memory_space=pltpu.VMEM)
    return pl.pallas_call(
        kernel,
        out_shape=[jax.ShapeDtypeStruct(s, F32) for s in shapes],
        in_specs=[smem] * scalars + [vmem] * (len(args) - scalars),
        out_specs=[vmem] * len(shapes),
        compiler_params=pltpu.CompilerParams(vmem_limit_bytes=28 * 2**20),
    )(*args)


def prepare_kernel(mask_ref, place_ref, f_ref, l32_ref, away_ref, home_ref, send_ref, wide_ref):
    side = lax.rem(place_ref[1], 2)

    def lower(r, c):
        return jnp.where(mask_ref[c, r] == 1, f_ref[tile(r, c), :], 0.0)

    x = lower(3, 2)
    l32_ref[...] = x
    l2 = [lower(2, s) for s in range(2)]
    l3 = [lower(3, s) for s in range(2)]
    for k in range(N):
        send_ref[k] = l2[k % 2]
    for k in range(N // 2):
        wide_ref[k] = x
    root, diag = f_ref[tile(3, 3), :], f_ref[tile(2, 2), :]
    away_ref[0] = home_ref[0] = root
    away_ref[1] = home_ref[1] = diag
    even = side == 0
    home_ref[2] = jnp.where(even, l2[0], l2[1])
    away_ref[2] = jnp.where(even, l2[1], l2[0])
    home_ref[3] = jnp.where(even, l3[0], l3[1])
    away_ref[3] = jnp.where(even, l3[1], l3[0])


def pack_kernel(place_ref, home_ref, got_ref, packed_ref, l3_ref):
    side = lax.rem(place_ref[1], 2)
    for i in range(3):
        packed_ref[i, side] = home_ref[i]
        packed_ref[i, 1 - side] = got_ref[i]
    l3_ref[side] = home_ref[3]
    l3_ref[1 - side] = got_ref[3]


def places(place_ref, d):
    layer, core = place_ref[0] // 2, lax.rem(place_ref[0], 2)
    k = lax.rem(layer + d, LAYERS) * 2
    return k + core, k + 1 - core


def t_kernel(place_ref, mine_ref, other_ref, l2_ref, l3_ref, t_ref, send_ref):
    total = jnp.zeros((2 * TB, TB), F32)
    for d in range(LAYERS):
        k0, k1 = places(place_ref, d)
        a = rows(*(lanes(mine_ref[d, i], other_ref[d, i]) for i in range(2)))
        total += dot3(split(a), split(rows(l2_ref[k0], l2_ref[k1])))
    for i in range(2):
        x = total[i * TB : (i + 1) * TB] - l3_ref[i]
        t_ref[i] = x
        for k in range(N // 2):
            send_ref[k, i] = x


def pair_rows(rows_ref, k0, k1, i):
    return rows(*(lanes(rows_ref[k0, i, j], rows_ref[k1, i, j]) for j in range(2)))


def uq_kernel(place_ref, rows_ref, l2_ref, l32_ref, u_ref, home_ref, away_ref):
    side = lax.rem(place_ref[1], 2)
    u = jnp.zeros((2 * TB, TB), F32)
    q = jnp.zeros((2 * TB, TB), F32)
    for k in range(0, N, 2):
        b = split(rows(l2_ref[k], l2_ref[k + 1]))
        u += dot3(split(pair_rows(rows_ref, k, k + 1, 1)), b)
    for i in range(0, N // 2, 2):
        k = 2 * i + side
        b = split(rows(l32_ref[i], l32_ref[i + 1]))
        q += dot3(split(pair_rows(rows_ref, k, k + 2, 0)), b)
    for i in range(2):
        u_ref[i] = u[i * TB : (i + 1) * TB]
    even = side == 0
    home_ref[...] = jnp.where(even, q[:TB], q[TB:])
    away_ref[...] = jnp.where(even, q[TB:], q[:TB])


def y_kernel(place_ref, rows_ref, t_ref, y_ref, home_ref, away_ref):
    side = lax.rem(place_ref[1], 2)
    y = jnp.zeros((2 * TB, TB), F32)
    for k in range(0, N, 2):
        b = split(rows(t_ref[k // 2, 0], t_ref[k // 2, 1]))
        y += dot3(split(pair_rows(rows_ref, k, k + 1, 0)), b)
    y_ref[...] = y
    even = side == 0
    home_ref[...] = jnp.where(even, y[:TB], y[TB:])
    away_ref[...] = jnp.where(even, y[TB:], y[:TB])


def sums_kernel(
    place_ref, y_ref, u_ref, q_home_ref, q_away_ref, l_mine_ref, l_other_ref, t_mine_ref, t_other_ref, rows_ref, sum_ref
):
    row = place_ref[1]
    side = lax.rem(row, 2)
    y = y_ref[...].T
    u = [u_ref[i].T for i in range(2)]
    y_split = split(y)
    yu_split = split(lanes(y, *u))
    q_split = split((q_home_ref[...] + q_away_ref[...]).T)
    for d in range(LAYERS):
        ks = places(place_ref, d)
        l32 = rows(*(lanes(l_mine_ref[d, i], l_other_ref[d, i]) for i in range(2)))
        l32_own = lanes(l_mine_ref[d, side], l_other_ref[d, side])
        low = [lanes(t_mine_ref[d, i], t_other_ref[d, i]) for i in range(2)]
        low += [lanes(rows_ref[ks[0], 2, i], rows_ref[ks[1], 2, i]) for i in range(2)]
        parts = [
            dot3(y_split, split(l32)),
            dot3(yu_split, split(rows(*low))),
            dot3(q_split, split(l32_own)),
        ]
        for j, part in enumerate(parts):
            for i, k in enumerate(ks):
                sum_ref[k, j] = part[:, i * TB : (i + 1) * TB]
    for i in range(2):
        sum_ref[row - side + i, 0] += u[i]


def finish_kernel(mask_ref, place_ref, f_ref, got_ref, home_ref, away_ref, q_home_ref, q_away_ref, out_ref):
    even = lax.rem(place_ref[1], 2) == 0

    def total(i, ks):
        x = got_ref[ks[0], i]
        for k in ks[1:]:
            x += got_ref[k, i]
        return x.T

    def masked(s, r, x):
        return jnp.where(mask_ref[s, r] == 1, x, 0.0)

    empty = jnp.zeros((TB, TB), F32)
    for r, c in ((0, 1), (0, 2), (0, 3), (1, 0), (1, 2), (1, 3), (2, 3)):
        out_ref[tile(r, c), :] = empty
    home, away = home_ref[...], away_ref[...]
    y = [jnp.where(even, home, away), jnp.where(even, away, home)]
    for s in range(2):
        ks = range(s, N, 2)
        out_ref[tile(s, s), :] = f_ref[tile(s, s), :] + total(1, ks)
        out_ref[tile(2, s), :] = masked(s, 2, -total(0, ks))
        out_ref[tile(3, s), :] = masked(s, 3, y[s])
    out_ref[tile(2, 2), :] = f_ref[tile(2, 2), :] + total(2, range(N))
    out_ref[tile(3, 2), :] = masked(2, 3, -(q_home_ref[...] + q_away_ref[...]))
    out_ref[tile(3, 3), :] = f_ref[tile(3, 3), :]


def gather_layers(x, ties):
    found = {0: x}
    up = down = x
    tied = []
    for step in range(1, LAYERS // 2):
        up = lax.ppermute(up, "col", LAYER_UP)
        down = lax.ppermute(down, "col", LAYER_DOWN)
        if step in ties:
            up, down, other = lax.optimization_barrier((up, down, ties[step]))
            tied.append(other)
        found[LAYERS - step] = up
        found[step] = down
    half = TB // 2
    found[LAYERS // 2] = jnp.concatenate(
        [
            lax.ppermute(up[:, :half], "col", LAYER_UP),
            lax.ppermute(down[:, half:], "col", LAYER_DOWN),
        ],
        axis=1,
    )
    mine = jnp.stack([found[d] for d in range(LAYERS)])
    if LAYERS // 2 in ties:
        mine, other = lax.optimization_barrier((mine, ties[LAYERS // 2]))
        tied.append(other)
    return (mine, lax.ppermute(mine, "col", CORE_SWAP), *tied)


def body(factor, structure):
    row = lax.axis_index("row")
    col = lax.axis_index("col")
    place = jnp.stack([col, row]).astype(jnp.int32)
    mask = structure.reshape(4, 4, N)
    mask = lax.dynamic_index_in_dim(mask, row, axis=2, keepdims=False)
    flat = factor.reshape(N * TB, TB)
    square = (TB, TB)

    with jax.named_scope("prepare"):
        l32, away, home, send, wide = call(
            prepare_kernel,
            [square, (4, *square), (4, *square), (N, *square), (N // 2, *square)],
            mask,
            place,
            flat,
            scalars=2,
        )
    with jax.named_scope("swap_l32"):
        l32_away = lax.ppermute(l32, "row", ROW_SWAP)
        even = lax.rem(row, 2) == 0
        l32_pair = jnp.stack([jnp.where(even, l32, l32_away), jnp.where(even, l32_away, l32)])
    with jax.named_scope("swap_rest"):
        l32_pair, away = lax.optimization_barrier((l32_pair, away))
        away = lax.ppermute(away, "row", ROW_SWAP)
    with jax.named_scope("gather_l2_cols"):
        send, wide, away = lax.optimization_barrier((send, wide, away))
        l2_cols = lax.all_to_all(send, "row", 0, 0, tiled=True)
    with jax.named_scope("gather_l32_cols"):
        l32_cols = lax.all_to_all(wide, "row", 0, 0, tiled=True, axis_index_groups=SAME_SIDE)
    with jax.named_scope("gather_l32_rows"):
        l_mine, l_other, away, l2_cols, l32_cols = gather_layers(
            l32_pair, {1: away, 3: l2_cols, 4: l32_cols}
        )
    with jax.named_scope("pack"):
        packed, l3 = call(pack_kernel, [(3, 2, *square), (2, *square)], place, home, away)
    with jax.named_scope("gather_rows"):
        panels = lax.all_gather(packed, "col", axis=0)
    with jax.named_scope("term_t"):
        t, send = call(
            t_kernel, [(2, *square), (N // 2, 2, *square)], place, l_mine, l_other, l2_cols, l3
        )
    with jax.named_scope("gather_t_cols"):
        t_cols = lax.all_to_all(send, "row", 0, 0, tiled=True, axis_index_groups=SAME_SIDE)
    with jax.named_scope("term_uq"):
        u, q_home, q_away = call(
            uq_kernel, [(2, *square), square, square], place, panels, l2_cols, l32_cols
        )
    with jax.named_scope("swap_q"):
        t_cols, q_away = lax.optimization_barrier((t_cols, q_away))
        q_away = lax.ppermute(q_away, "row", ROW_SWAP)
    with jax.named_scope("gather_t_rows"):
        t_mine, t_other, (t_cols, u, q_home), q_away = gather_layers(
            t, {3: (t_cols, u, q_home), 4: q_away}
        )
    with jax.named_scope("term_y"):
        y, y_home, y_away = call(
            y_kernel, [(2 * TB, TB), square, square], place, panels, t_cols
        )
    with jax.named_scope("swap_y"):
        y_away = lax.ppermute(y_away, "row", ROW_SWAP)
    with jax.named_scope("sums"):
        (sums,) = call(
            sums_kernel,
            [(N, 3, *square)],
            place,
            y,
            u,
            q_home,
            q_away,
            l_mine,
            l_other,
            t_mine,
            t_other,
            panels,
        )
    with jax.named_scope("scatter_sums"):
        sums, y_away = lax.optimization_barrier((sums, y_away))
        got = lax.all_to_all(sums, "row", 0, 0, tiled=True)
    with jax.named_scope("finish"):
        (out,) = call(
            finish_kernel,
            [(N * TB, TB)],
            mask,
            place,
            flat,
            got,
            y_home,
            y_away,
            q_home,
            q_away,
            scalars=2,
        )
        return out.reshape(factor.shape)


def solution(mesh):
    return jax.shard_map(
        body,
        mesh=mesh,
        in_specs=(P(None, "row", None, "col"), P()),
        out_specs=P(None, "row", None, "col"),
        check_vma=False,
    )
```

```python
import jax
import jax.numpy as jnp
from jax import lax
from jax.experimental import pallas as pl
from jax.experimental.pallas import tpu as pltpu
from jax.sharding import PartitionSpec as P

N = 16
LAYERS = 8
TB = 128
F32 = jnp.float32
BF16 = jnp.bfloat16
CORE_SWAP = [(i, i ^ 1) for i in range(N)]
ROW_SWAP = [(i, i ^ 1) for i in range(N)]
SAME_SIDE = [[p + 2 * i for i in range(N // 2)] for p in range(2)]
LAYER_UP = [(i, (i + 2) % N) for i in range(N)]
LAYER_DOWN = [(i, (i - 2) % N) for i in range(N)]


def split(x):
    high = x.astype(BF16)
    return high, (x - high.astype(F32)).astype(BF16)


def dot3(a, b):
    a_high, a_low = a
    b_high, b_low = b

    def one(x, y):
        return jnp.dot(x, y, preferred_element_type=F32)

    return one(a_high, b_high) + (one(a_high, b_low) + one(a_low, b_high))


def lanes(*tiles):
    return jnp.concatenate(tiles, axis=1)


def rows(*tiles):
    return jnp.concatenate(tiles, axis=0)


def tile(r, c):
    return pl.ds(r * 4 * TB + c, TB, stride=4)


def call(kernel, shapes, *args, scalars=1):
    smem = pl.BlockSpec(memory_space=pltpu.SMEM)
    vmem = pl.BlockSpec(memory_space=pltpu.VMEM)
    return pl.pallas_call(
        kernel,
        out_shape=[jax.ShapeDtypeStruct(s, F32) for s in shapes],
        in_specs=[smem] * scalars + [vmem] * (len(args) - scalars),
        out_specs=[vmem] * len(shapes),
        compiler_params=pltpu.CompilerParams(vmem_limit_bytes=28 * 2**20),
    )(*args)


def prepare_kernel(mask_ref, place_ref, f_ref, l32_ref, away_ref, home_ref, send_ref, wide_ref):
    side = lax.rem(place_ref[1], 2)

    def lower(r, c):
        return jnp.where(mask_ref[c, r] == 1, f_ref[tile(r, c), :], 0.0)

    x = lower(3, 2)
    l32_ref[...] = x
    l2 = [lower(2, s) for s in range(2)]
    l3 = [lower(3, s) for s in range(2)]
    for k in range(N):
        send_ref[k] = l2[k % 2]
    for k in range(N // 2):
        wide_ref[k] = x
    root, diag = f_ref[tile(3, 3), :], f_ref[tile(2, 2), :]
    away_ref[0] = home_ref[0] = root
    away_ref[1] = home_ref[1] = diag
    even = side == 0
    home_ref[2] = jnp.where(even, l2[0], l2[1])
    away_ref[2] = jnp.where(even, l2[1], l2[0])
    home_ref[3] = jnp.where(even, l3[0], l3[1])
    away_ref[3] = jnp.where(even, l3[1], l3[0])


def pack_kernel(place_ref, home_ref, got_ref, packed_ref, l3_ref):
    side = lax.rem(place_ref[1], 2)
    for i in range(3):
        packed_ref[i, side] = home_ref[i]
        packed_ref[i, 1 - side] = got_ref[i]
    l3_ref[side] = home_ref[3]
    l3_ref[1 - side] = got_ref[3]


def places(place_ref, d):
    layer, core = place_ref[0] // 2, lax.rem(place_ref[0], 2)
    k = lax.rem(layer + d, LAYERS) * 2
    return k + core, k + 1 - core


def t_kernel(place_ref, *refs):
    mine, other = refs[:LAYERS], refs[LAYERS : 2 * LAYERS]
    l2_ref, l3_ref, t_ref, send_ref = refs[2 * LAYERS :]
    total = jnp.zeros((2 * TB, TB), F32)
    for d in range(LAYERS):
        k0, k1 = places(place_ref, d)
        a = rows(*(lanes(mine[d][i], other[d][i]) for i in range(2)))
        total += dot3(split(a), split(rows(l2_ref[k0], l2_ref[k1])))
    for i in range(2):
        x = total[i * TB : (i + 1) * TB] - l3_ref[i]
        t_ref[i] = x
        for k in range(N // 2):
            send_ref[k, i] = x


def pair_rows(rows_ref, k0, k1, i):
    return rows(*(lanes(rows_ref[k0, i, j], rows_ref[k1, i, j]) for j in range(2)))


def uq_kernel(place_ref, rows_ref, l2_ref, l32_ref, u_ref, home_ref, away_ref):
    side = lax.rem(place_ref[1], 2)
    u = jnp.zeros((2 * TB, TB), F32)
    q = jnp.zeros((2 * TB, TB), F32)
    for k in range(0, N, 2):
        b = split(rows(l2_ref[k], l2_ref[k + 1]))
        u += dot3(split(pair_rows(rows_ref, k, k + 1, 1)), b)
    for i in range(0, N // 2, 2):
        k = 2 * i + side
        b = split(rows(l32_ref[i], l32_ref[i + 1]))
        q += dot3(split(pair_rows(rows_ref, k, k + 2, 0)), b)
    for i in range(2):
        u_ref[i] = u[i * TB : (i + 1) * TB]
    even = side == 0
    home_ref[...] = jnp.where(even, q[:TB], q[TB:])
    away_ref[...] = jnp.where(even, q[TB:], q[:TB])


def y_kernel(place_ref, rows_ref, t_ref, y_ref, home_ref, away_ref):
    side = lax.rem(place_ref[1], 2)
    y = jnp.zeros((2 * TB, TB), F32)
    for k in range(0, N, 2):
        b = split(rows(t_ref[k // 2, 0], t_ref[k // 2, 1]))
        y += dot3(split(pair_rows(rows_ref, k, k + 1, 0)), b)
    y_ref[...] = y
    even = side == 0
    home_ref[...] = jnp.where(even, y[:TB], y[TB:])
    away_ref[...] = jnp.where(even, y[TB:], y[:TB])


def sums_kernel(place_ref, *refs):
    l_mine, l_other, t_mine, t_other = (refs[i * LAYERS : (i + 1) * LAYERS] for i in range(4))
    y_ref, u_ref, q_home_ref, q_away_ref, rows_ref, sum_ref = refs[4 * LAYERS :]
    row = place_ref[1]
    side = lax.rem(row, 2)
    y = y_ref[...].T
    u = [u_ref[i].T for i in range(2)]
    y_split = split(y)
    yu_split = split(lanes(y, *u))
    q_split = split((q_home_ref[...] + q_away_ref[...]).T)
    for d in range(LAYERS):
        ks = places(place_ref, d)
        l32 = rows(*(lanes(l_mine[d][i], l_other[d][i]) for i in range(2)))
        l32_own = lanes(l_mine[d][side], l_other[d][side])
        low = [lanes(t_mine[d][i], t_other[d][i]) for i in range(2)]
        low += [lanes(rows_ref[ks[0], 2, i], rows_ref[ks[1], 2, i]) for i in range(2)]
        parts = [
            dot3(y_split, split(l32)),
            dot3(yu_split, split(rows(*low))),
            dot3(q_split, split(l32_own)),
        ]
        for j, part in enumerate(parts):
            for i, k in enumerate(ks):
                sum_ref[k, j] = part[:, i * TB : (i + 1) * TB]
    for i in range(2):
        sum_ref[row - side + i, 0] += u[i]


def finish_kernel(mask_ref, place_ref, f_ref, got_ref, home_ref, away_ref, q_home_ref, q_away_ref, out_ref):
    even = lax.rem(place_ref[1], 2) == 0

    def total(i, ks):
        x = got_ref[ks[0], i]
        for k in ks[1:]:
            x += got_ref[k, i]
        return x.T

    def masked(s, r, x):
        return jnp.where(mask_ref[s, r] == 1, x, 0.0)

    empty = jnp.zeros((TB, TB), F32)
    for r, c in ((0, 1), (0, 2), (0, 3), (1, 0), (1, 2), (1, 3), (2, 3)):
        out_ref[tile(r, c), :] = empty
    home, away = home_ref[...], away_ref[...]
    y = [jnp.where(even, home, away), jnp.where(even, away, home)]
    for s in range(2):
        ks = range(s, N, 2)
        out_ref[tile(s, s), :] = f_ref[tile(s, s), :] + total(1, ks)
        out_ref[tile(2, s), :] = masked(s, 2, -total(0, ks))
        out_ref[tile(3, s), :] = masked(s, 3, y[s])
    out_ref[tile(2, 2), :] = f_ref[tile(2, 2), :] + total(2, range(N))
    out_ref[tile(3, 2), :] = masked(2, 3, -(q_home_ref[...] + q_away_ref[...]))
    out_ref[tile(3, 3), :] = f_ref[tile(3, 3), :]


def swap_cores(x):
    return lax.ppermute(x, "col", CORE_SWAP)


def gather_layers(x, ties):
    mine = {0: x}
    other = {}
    late = [0]
    up = down = x
    tied = []
    last = LAYERS // 2
    for step in range(1, last + 1):
        swapped = [swap_cores(mine[d]) for d in late]
        up = lax.ppermute(up, "col", LAYER_UP)
        if step < last:
            down = lax.ppermute(down, "col", LAYER_DOWN)
        up, down, swapped, more = lax.optimization_barrier((up, down, swapped, ties.get(step)))
        tied.append(more)
        other.update(zip(late, swapped))
        mine[LAYERS - step] = up
        late = [LAYERS - step]
        if step < last:
            mine[step] = down
            late.append(step)
    swapped, more = lax.optimization_barrier((swap_cores(up), ties.get(last + 1)))
    tied.append(more)
    other[last] = swapped
    order = range(LAYERS)
    return [mine[d] for d in order], [other[d] for d in order], [t for t in tied if t is not None]


def body(factor, structure):
    row = lax.axis_index("row")
    col = lax.axis_index("col")
    place = jnp.stack([col, row]).astype(jnp.int32)
    mask = structure.reshape(4, 4, N)
    mask = lax.dynamic_index_in_dim(mask, row, axis=2, keepdims=False)
    flat = factor.reshape(N * TB, TB)
    square = (TB, TB)

    with jax.named_scope("prepare"):
        l32, away, home, send, wide = call(
            prepare_kernel,
            [square, (4, *square), (4, *square), (N, *square), (N // 2, *square)],
            mask,
            place,
            flat,
            scalars=2,
        )
    with jax.named_scope("swap_l32"):
        l32_away = lax.ppermute(l32, "row", ROW_SWAP)
        even = lax.rem(row, 2) == 0
        l32_pair = jnp.stack([jnp.where(even, l32, l32_away), jnp.where(even, l32_away, l32)])
    with jax.named_scope("swap_rest"):
        l32_pair, away = lax.optimization_barrier((l32_pair, away))
        away = lax.ppermute(away, "row", ROW_SWAP)
    with jax.named_scope("gather_l2_cols"):
        send, wide, away = lax.optimization_barrier((send, wide, away))
        l2_cols = lax.all_to_all(send, "row", 0, 0, tiled=True)
    with jax.named_scope("gather_l32_cols"):
        l32_cols = lax.all_to_all(wide, "row", 0, 0, tiled=True, axis_index_groups=SAME_SIDE)
    with jax.named_scope("gather_l32_rows"):
        l_mine, l_other, (away, l2_cols, l32_cols) = gather_layers(
            l32_pair, {1: away, 3: l2_cols, 5: l32_cols}
        )
    with jax.named_scope("pack"):
        packed, l3 = call(pack_kernel, [(3, 2, *square), (2, *square)], place, home, away)
    with jax.named_scope("gather_rows"):
        panels = lax.all_gather(packed, "col", axis=0)
    with jax.named_scope("term_t"):
        t, send = call(
            t_kernel, [(2, *square), (N // 2, 2, *square)], place, *l_mine, *l_other, l2_cols, l3
        )
    with jax.named_scope("gather_t_cols"):
        t_cols = lax.all_to_all(send, "row", 0, 0, tiled=True, axis_index_groups=SAME_SIDE)
    with jax.named_scope("term_uq"):
        u, q_home, q_away = call(
            uq_kernel, [(2, *square), square, square], place, panels, l2_cols, l32_cols
        )
    with jax.named_scope("swap_q"):
        q_away = lax.ppermute(q_away, "row", ROW_SWAP)
    with jax.named_scope("gather_t_rows"):
        t_mine, t_other, ((u, q_home), (t_cols, q_away)) = gather_layers(
            t, {3: (u, q_home), 4: (t_cols, q_away)}
        )
    with jax.named_scope("term_y"):
        y, y_home, y_away = call(
            y_kernel, [(2 * TB, TB), square, square], place, panels, t_cols
        )
    with jax.named_scope("swap_y"):
        y_away = lax.ppermute(y_away, "row", ROW_SWAP)
    with jax.named_scope("sums"):
        (sums,) = call(
            sums_kernel,
            [(N, 3, *square)],
            place,
            *l_mine,
            *l_other,
            *t_mine,
            *t_other,
            y,
            u,
            q_home,
            q_away,
            panels,
        )
    with jax.named_scope("scatter_sums"):
        sums, y_away = lax.optimization_barrier((sums, y_away))
        got = lax.all_to_all(sums, "row", 0, 0, tiled=True)
    with jax.named_scope("finish"):
        (out,) = call(
            finish_kernel,
            [(N * TB, TB)],
            mask,
            place,
            flat,
            got,
            y_home,
            y_away,
            q_home,
            q_away,
            scalars=2,
        )
        return out.reshape(factor.shape)


def solution(mesh):
    return jax.shard_map(
        body,
        mesh=mesh,
        in_specs=(P(None, "row", None, "col"), P()),
        out_specs=P(None, "row", None, "col"),
        check_vma=False,
    )
```

```python
import jax
import jax.numpy as jnp
from jax import lax
from jax.experimental import pallas as pl
from jax.experimental.pallas import tpu as pltpu
from jax.sharding import PartitionSpec as P

N = 16
LAYERS = 8
TB = 128
HALF = 64
F32 = jnp.float32
BF16 = jnp.bfloat16
CORE_SWAP = [(i, i ^ 1) for i in range(N)]
ROW_SWAP = [(i, i ^ 1) for i in range(N)]
SAME_SIDE = [[p + 2 * i for i in range(N // 2)] for p in range(2)]
LAYER_UP = [(i, (i + 2) % N) for i in range(N)]
LAYER_DOWN = [(i, (i - 2) % N) for i in range(N)]


def split(x):
    high = x.astype(BF16)
    return high, (x - high.astype(F32)).astype(BF16)


def dot3(a, b):
    a_high, a_low = a
    b_high, b_low = b

    def one(x, y):
        return jnp.dot(x, y, preferred_element_type=F32)

    return one(a_high, b_high) + (one(a_high, b_low) + one(a_low, b_high))


def lanes(*tiles):
    return jnp.concatenate(tiles, axis=1)


def rows(*tiles):
    return jnp.concatenate(tiles, axis=0)


def tile(r, c):
    return pl.ds(r * 4 * TB + c, TB, stride=4)


def call(kernel, shapes, *args, scalars=1):
    smem = pl.BlockSpec(memory_space=pltpu.SMEM)
    vmem = pl.BlockSpec(memory_space=pltpu.VMEM)
    return pl.pallas_call(
        kernel,
        out_shape=[jax.ShapeDtypeStruct(s, F32) for s in shapes],
        in_specs=[smem] * scalars + [vmem] * (len(args) - scalars),
        out_specs=[vmem] * len(shapes),
        compiler_params=pltpu.CompilerParams(vmem_limit_bytes=10 * 2**20),
    )(*args)


def prepare_kernel(mask_ref, place_ref, f_ref, l32_ref, away_ref, home_ref, send_ref):
    side = lax.rem(place_ref[1], 2)

    def lower(r, c):
        return jnp.where(mask_ref[c, r] == 1, f_ref[tile(r, c), :], 0.0)

    x = lower(3, 2)
    l32_ref[...] = x
    turned = x.T
    l2 = [lower(2, s) for s in range(2)]
    l3 = [lower(3, s) for s in range(2)]
    for k in range(N):
        send_ref[k, :TB] = l2[k % 2]
        send_ref[k, TB:] = turned[k % 2 * HALF : (k % 2 + 1) * HALF]
    root, diag = f_ref[tile(3, 3), :], f_ref[tile(2, 2), :]
    away_ref[0] = home_ref[0] = root
    away_ref[1] = home_ref[1] = diag
    even = side == 0
    home_ref[2] = jnp.where(even, l2[0], l2[1])
    away_ref[2] = jnp.where(even, l2[1], l2[0])
    home_ref[3] = jnp.where(even, l3[0], l3[1])
    away_ref[3] = jnp.where(even, l3[1], l3[0])


def pack_kernel(place_ref, home_ref, got_ref, packed_ref, l3_ref):
    side = lax.rem(place_ref[1], 2)
    for i in range(3):
        packed_ref[i, side] = home_ref[i]
        packed_ref[i, 1 - side] = got_ref[i]
    l3_ref[side] = home_ref[3]
    l3_ref[1 - side] = got_ref[3]


def places(place_ref, d):
    layer, core = place_ref[0] // 2, lax.rem(place_ref[0], 2)
    k = lax.rem(layer + d, LAYERS) * 2
    return k + core, k + 1 - core


def t_kernel(place_ref, *refs):
    mine, other = refs[:LAYERS], refs[LAYERS : 2 * LAYERS]
    l2_ref, l3_ref, t_ref, send_ref, all_ref = refs[2 * LAYERS :]
    total = jnp.zeros((2 * TB, TB), F32)
    for d in range(LAYERS):
        k0, k1 = places(place_ref, d)
        a = rows(*(lanes(mine[d][i], other[d][i]) for i in range(2)))
        all_ref[d] = a
        total += dot3(split(a), split(rows(l2_ref[k0, :TB], l2_ref[k1, :TB])))
    for i in range(2):
        x = total[i * TB : (i + 1) * TB] - l3_ref[i]
        t_ref[i] = x
        for k in range(N // 2):
            send_ref[k, i] = x


def pair_rows(rows_ref, k):
    return rows(*(lanes(rows_ref[k, j], rows_ref[k + 1, j]) for j in range(2)))


def dot3_turned(a, b):
    def one(x, y):
        return lax.dot_general(x, y, (((1,), (1,)), ((), ())), preferred_element_type=F32)

    return one(a[0], b[0]) + (one(a[0], b[1]) + one(a[1], b[0]))


def uq_kernel(place_ref, root_ref, diag_ref, cols_ref, u_ref, q_ref, home_ref, away_ref):
    u = jnp.zeros((2 * TB, TB), F32)
    q = jnp.zeros((HALF, 2 * TB), F32)
    for k in range(0, N, 2):
        b = split(rows(cols_ref[k, :TB], cols_ref[k + 1, :TB]))
        u += dot3(split(pair_rows(diag_ref, k)), b)
        b = split(lanes(cols_ref[k, TB:], cols_ref[k + 1, TB:]))
        q += dot3_turned(b, split(pair_rows(root_ref, k)))
    for i in range(2):
        u_ref[i] = u[i * TB : (i + 1) * TB]
    q_ref[...] = q
    even = lax.rem(place_ref[1], 2) == 0
    home_ref[...] = jnp.where(even, q[:, :TB], q[:, TB:])
    away_ref[...] = jnp.where(even, q[:, TB:], q[:, :TB])


def y_kernel(place_ref, root_ref, t_ref, y_ref, home_ref, away_ref):
    y = jnp.zeros((2 * TB, TB), F32)
    for k in range(0, N, 2):
        b = split(rows(t_ref[k // 2, 0], t_ref[k // 2, 1]))
        y += dot3(split(pair_rows(root_ref, k)), b)
    y_ref[...] = y
    even = lax.rem(place_ref[1], 2) == 0
    home_ref[...] = jnp.where(even, y[:TB], y[TB:])
    away_ref[...] = jnp.where(even, y[TB:], y[:TB])


def sums_kernel(place_ref, *refs):
    t_mine, t_other = refs[:LAYERS], refs[LAYERS : 2 * LAYERS]
    l32_ref, y_ref, u_ref, q_ref, l2_ref, sum_ref = refs[2 * LAYERS :]
    row = place_ref[1]
    side = lax.rem(row, 2)
    y = y_ref[...].T
    u = [u_ref[i].T for i in range(2)]
    left = split(rows(y, q_ref[...]))
    yu_split = split(lanes(y, *u))
    for d in range(LAYERS):
        ks = places(place_ref, d)
        low = [lanes(t_mine[d][i], t_other[d][i]) for i in range(2)]
        low += [lanes(l2_ref[ks[0], i], l2_ref[ks[1], i]) for i in range(2)]
        x = dot3(left, split(l32_ref[d]))
        z = dot3(yu_split, split(rows(*low)))
        for i, k in enumerate(ks):
            at = slice(i * TB, (i + 1) * TB)
            sum_ref[k, :TB] = x[:TB, at]
            sum_ref[k, TB : 2 * TB] = z[:, at]
            sum_ref[k, 2 * TB :] = x[TB:, at]
    for i in range(2):
        sum_ref[row - side + i, :TB] += u[i]


def finish_kernel(
    mask_ref, place_ref, f_ref, got_ref, home_ref, away_ref, q_home_ref, q_away_ref, out_ref
):
    even = lax.rem(place_ref[1], 2) == 0

    def masked(s, r, x):
        return jnp.where(mask_ref[s, r] == 1, x, 0.0)

    def both(home, away):
        return [jnp.where(even, home, away), jnp.where(even, away, home)]

    empty = jnp.zeros((TB, TB), F32)
    for r, c in ((0, 1), (0, 2), (0, 3), (1, 0), (1, 2), (1, 3), (2, 3)):
        out_ref[tile(r, c), :] = empty
    y = both(home_ref[...], away_ref[...])
    q = rows(*both(q_home_ref[...], q_away_ref[...])).T
    parts = []
    for s in range(2):
        total = got_ref[s]
        for k in range(s + 2, N, 2):
            total += got_ref[k]
        out_ref[tile(s, s), :] = f_ref[tile(s, s), :] + total[TB : 2 * TB].T
        out_ref[tile(2, s), :] = masked(s, 2, -total[:TB].T)
        out_ref[tile(3, s), :] = masked(s, 3, y[s])
        parts.append(total[2 * TB :])
    out_ref[tile(2, 2), :] = f_ref[tile(2, 2), :] + rows(*parts).T
    out_ref[tile(3, 2), :] = masked(2, 3, -q)
    out_ref[tile(3, 3), :] = f_ref[tile(3, 3), :]


def swap_cores(x):
    return lax.ppermute(x, "col", CORE_SWAP)


def gather_layers(x, begin, ties):
    mine = {0: x}
    other = {}
    late = [0]
    up = down = x
    tied = []
    last = LAYERS // 2
    half = TB // 2
    beside = None
    for step in range(1, last + 1):
        swapped = [swap_cores(mine[d]) for d in late]
        if step == begin[0]:
            swapped, operand = lax.optimization_barrier((swapped, begin[1]))
            beside = begin[2](operand)
        if step == last:
            up, down = up[:, :half], down[:, half:]
        up = lax.ppermute(up, "col", LAYER_UP)
        down = lax.ppermute(down, "col", LAYER_DOWN)
        up, down, swapped, more = lax.optimization_barrier((up, down, swapped, ties.get(step)))
        tied.append(more)
        other.update(zip(late, swapped))
        if step < last:
            mine[LAYERS - step], mine[step] = up, down
            late = [LAYERS - step, step]
    mine[last] = jnp.concatenate([up, down], axis=1)
    other[last], beside = lax.optimization_barrier((swap_cores(mine[last]), beside))
    order = range(LAYERS)
    return [mine[d] for d in order], [other[d] for d in order], beside, *(t for t in tied if t is not None)


def body(factor, structure):
    row = lax.axis_index("row")
    col = lax.axis_index("col")
    place = jnp.stack([col, row]).astype(jnp.int32)
    mask = structure.reshape(4, 4, N)
    mask = lax.dynamic_index_in_dim(mask, row, axis=2, keepdims=False)
    flat = factor.reshape(N * TB, TB)
    square = (TB, TB)

    def to_rows(x):
        return lax.all_to_all(x, "row", 0, 0, tiled=True)

    def to_side(x):
        return lax.all_to_all(x, "row", 0, 0, tiled=True, axis_index_groups=SAME_SIDE)

    with jax.named_scope("prepare"):
        l32, away, home, send = call(
            prepare_kernel,
            [square, (4, *square), (4, *square), (N, TB + HALF, TB)],
            mask,
            place,
            flat,
            scalars=2,
        )
    with jax.named_scope("swap_l32"):
        l32_away = lax.ppermute(l32, "row", ROW_SWAP)
        even = lax.rem(row, 2) == 0
        l32_pair = jnp.stack([jnp.where(even, l32, l32_away), jnp.where(even, l32_away, l32)])
    with jax.named_scope("swap_rest"):
        l32_pair, away = lax.optimization_barrier((l32_pair, away))
        away = lax.ppermute(away, "row", ROW_SWAP)
    with jax.named_scope("gather_l"):
        l_mine, l_other, cols, away = gather_layers(l32_pair, (2, send, to_rows), {1: away})
    with jax.named_scope("pack"):
        packed, l3 = call(pack_kernel, [(3, 2, *square), (2, *square)], place, home, away)
    with jax.named_scope("gather_rows"):
        panels = lax.all_gather(packed, "col", axis=0)
        root_rows, diag_rows, l2_rows = (panels[:, i] for i in range(3))
    with jax.named_scope("term_t"):
        t, send, l32_rows = call(
            t_kernel,
            [(2, *square), (N // 2, 2, *square), (LAYERS, 2 * TB, 2 * TB)],
            place,
            *l_mine,
            *l_other,
            cols,
            l3,
        )
    with jax.named_scope("term_uq"):
        u, q, q_home, q_away = call(
            uq_kernel,
            [(2, *square), (HALF, 2 * TB), (HALF, TB), (HALF, TB)],
            place,
            root_rows,
            diag_rows,
            cols,
        )
    with jax.named_scope("gather_t"):
        t_mine, t_other, t_cols, (u, q) = gather_layers(t, (1, send, to_side), {3: (u, q)})
    with jax.named_scope("term_y"):
        y, y_home, y_away = call(
            y_kernel, [(2 * TB, TB), square, square], place, root_rows, t_cols
        )
    with jax.named_scope("swap_yq"):
        away = jnp.concatenate([y_away, q_away])
        away = lax.ppermute(away, "row", ROW_SWAP)
        y_away, q_away = away[:TB], away[TB:]
    with jax.named_scope("sums"):
        (sums,) = call(
            sums_kernel,
            [(N, 2 * TB + HALF, TB)],
            place,
            *t_mine,
            *t_other,
            l32_rows,
            y,
            u,
            q,
            l2_rows,
        )
    with jax.named_scope("scatter_sums"):
        sums, y_away, q_away = lax.optimization_barrier((sums, y_away, q_away))
        got = lax.all_to_all(sums, "row", 0, 0, tiled=True)
    with jax.named_scope("finish"):
        (out,) = call(
            finish_kernel,
            [(N * TB, TB)],
            mask,
            place,
            flat,
            got,
            y_home,
            y_away,
            q_home,
            q_away,
            scalars=2,
        )
        return out.reshape(factor.shape)


def solution(mesh):
    return jax.shard_map(
        body,
        mesh=mesh,
        in_specs=(P(None, "row", None, "col"), P()),
        out_specs=P(None, "row", None, "col"),
        check_vma=False,
    )
```

```python
import jax
import jax.numpy as jnp
from jax import lax
from jax.experimental import pallas as pl
from jax.experimental.pallas import tpu as pltpu
from jax.sharding import PartitionSpec as P

N = 16
LAYERS = 8
TB = 128
HALF = 64
F32 = jnp.float32
BF16 = jnp.bfloat16
CORE_SWAP = [(i, i ^ 1) for i in range(N)]
ROW_SWAP = [(i, i ^ 1) for i in range(N)]
SAME_SIDE = [[p + 2 * i for i in range(N // 2)] for p in range(2)]
LAYER_UP = [(i, (i + 2) % N) for i in range(N)]
LAYER_DOWN = [(i, (i - 2) % N) for i in range(N)]


def split(x):
    high = x.astype(BF16)
    return high, (x - high.astype(F32)).astype(BF16)


def dot3(a, b):
    a_high, a_low = a
    b_high, b_low = b

    def one(x, y):
        return jnp.dot(x, y, preferred_element_type=F32)

    return one(a_high, b_high) + (one(a_high, b_low) + one(a_low, b_high))


def lanes(*tiles):
    return jnp.concatenate(tiles, axis=1)


def rows(*tiles):
    return jnp.concatenate(tiles, axis=0)


def tile(r, c):
    return pl.ds(r * 4 * TB + c, TB, stride=4)


def call(kernel, shapes, *args, scalars=1):
    smem = pl.BlockSpec(memory_space=pltpu.SMEM)
    vmem = pl.BlockSpec(memory_space=pltpu.VMEM)
    return pl.pallas_call(
        kernel,
        out_shape=[jax.ShapeDtypeStruct(s, F32) for s in shapes],
        in_specs=[smem] * scalars + [vmem] * (len(args) - scalars),
        out_specs=[vmem] * len(shapes),
        compiler_params=pltpu.CompilerParams(vmem_limit_bytes=5 * 2**20),
    )(*args)


def prepare_kernel(mask_ref, place_ref, f_ref, l32_ref, away_ref, home_ref, send_ref):
    side = lax.rem(place_ref[1], 2)

    def lower(r, c):
        return jnp.where(mask_ref[c, r] == 1, f_ref[tile(r, c), :], 0.0)

    x = lower(3, 2)
    l32_ref[...] = x
    turned = x.T
    l2 = [lower(2, s) for s in range(2)]
    l3 = [lower(3, s) for s in range(2)]
    for k in range(N):
        send_ref[k, :TB] = l2[k % 2]
        send_ref[k, TB:] = turned[k % 2 * HALF : (k % 2 + 1) * HALF]
    root, diag = f_ref[tile(3, 3), :], f_ref[tile(2, 2), :]
    away_ref[0] = home_ref[0] = root
    away_ref[1] = home_ref[1] = diag
    even = side == 0
    home_ref[2] = jnp.where(even, l2[0], l2[1])
    away_ref[2] = jnp.where(even, l2[1], l2[0])
    home_ref[3] = jnp.where(even, l3[0], l3[1])
    away_ref[3] = jnp.where(even, l3[1], l3[0])


def pack_kernel(place_ref, home_ref, got_ref, packed_ref, l3_ref):
    side = lax.rem(place_ref[1], 2)
    for i in range(3):
        packed_ref[i, side] = home_ref[i]
        packed_ref[i, 1 - side] = got_ref[i]
    l3_ref[side] = home_ref[3]
    l3_ref[1 - side] = got_ref[3]


def places(place_ref, d):
    layer, core = place_ref[0] // 2, lax.rem(place_ref[0], 2)
    k = lax.rem(layer + d, LAYERS) * 2
    return k + core, k + 1 - core


def t_kernel(place_ref, *refs):
    mine, other = refs[:LAYERS], refs[LAYERS : 2 * LAYERS]
    l2_ref, l3_ref, t_ref, send_ref, all_ref = refs[2 * LAYERS :]
    total = jnp.zeros((2 * TB, TB), F32)
    for d in range(LAYERS):
        k0, k1 = places(place_ref, d)
        a = rows(*(lanes(mine[d][i], other[d][i]) for i in range(2)))
        all_ref[d] = a
        total += dot3(split(a), split(rows(l2_ref[k0, :TB], l2_ref[k1, :TB])))
    for i in range(2):
        x = total[i * TB : (i + 1) * TB] - l3_ref[i]
        t_ref[i] = x
        for k in range(N // 2):
            send_ref[k, i] = x


def pair_rows(rows_ref, k):
    return rows(*(lanes(rows_ref[k, j], rows_ref[k + 1, j]) for j in range(2)))


def dot3_turned(a, b):
    def one(x, y):
        return lax.dot_general(x, y, (((1,), (1,)), ((), ())), preferred_element_type=F32)

    return one(a[0], b[0]) + (one(a[0], b[1]) + one(a[1], b[0]))


def uq_kernel(place_ref, root_ref, diag_ref, cols_ref, u_ref, q_ref, home_ref, away_ref):
    u = jnp.zeros((2 * TB, TB), F32)
    q = jnp.zeros((HALF, 2 * TB), F32)
    for k in range(0, N, 2):
        b = split(rows(cols_ref[k, :TB], cols_ref[k + 1, :TB]))
        u += dot3(split(pair_rows(diag_ref, k)), b)
        b = split(lanes(cols_ref[k, TB:], cols_ref[k + 1, TB:]))
        q += dot3_turned(b, split(pair_rows(root_ref, k)))
    for i in range(2):
        u_ref[i] = u[i * TB : (i + 1) * TB]
    q_ref[...] = q
    even = lax.rem(place_ref[1], 2) == 0
    home_ref[...] = jnp.where(even, q[:, :TB], q[:, TB:])
    away_ref[...] = jnp.where(even, q[:, TB:], q[:, :TB])


def y_kernel(place_ref, root_ref, t_ref, y_ref, home_ref, away_ref):
    y = jnp.zeros((2 * TB, TB), F32)
    for k in range(0, N, 2):
        b = split(rows(t_ref[k // 2, 0], t_ref[k // 2, 1]))
        y += dot3(split(pair_rows(root_ref, k)), b)
    y_ref[...] = y
    even = lax.rem(place_ref[1], 2) == 0
    home_ref[...] = jnp.where(even, y[:TB], y[TB:])
    away_ref[...] = jnp.where(even, y[TB:], y[:TB])


def sums_kernel(place_ref, *refs):
    t_mine, t_other = refs[:LAYERS], refs[LAYERS : 2 * LAYERS]
    l32_ref, y_ref, u_ref, q_ref, l2_ref, sum_ref = refs[2 * LAYERS :]
    row = place_ref[1]
    side = lax.rem(row, 2)
    y = y_ref[...].T
    u = [u_ref[i].T for i in range(2)]
    left = split(rows(y, q_ref[...]))
    yu_split = split(lanes(y, *u))
    for d in range(LAYERS):
        ks = places(place_ref, d)
        low = [lanes(t_mine[d][i], t_other[d][i]) for i in range(2)]
        low += [lanes(l2_ref[ks[0], i], l2_ref[ks[1], i]) for i in range(2)]
        x = dot3(left, split(l32_ref[d]))
        z = dot3(yu_split, split(rows(*low)))
        for i, k in enumerate(ks):
            at = slice(i * TB, (i + 1) * TB)
            sum_ref[k, :TB] = x[:TB, at]
            sum_ref[k, TB : 2 * TB] = z[:, at]
            sum_ref[k, 2 * TB :] = x[TB:, at]
    for i in range(2):
        sum_ref[row - side + i, :TB] += u[i]


def finish_kernel(
    mask_ref, place_ref, f_ref, got_ref, home_ref, away_ref, q_home_ref, q_away_ref, out_ref
):
    even = lax.rem(place_ref[1], 2) == 0

    def masked(s, r, x):
        return jnp.where(mask_ref[s, r] == 1, x, 0.0)

    def both(home, away):
        return [jnp.where(even, home, away), jnp.where(even, away, home)]

    empty = jnp.zeros((TB, TB), F32)
    for r, c in ((0, 1), (0, 2), (0, 3), (1, 0), (1, 2), (1, 3), (2, 3)):
        out_ref[tile(r, c), :] = empty
    y = both(home_ref[...], away_ref[...])
    q = rows(*both(q_home_ref[...], q_away_ref[...])).T
    parts = []
    for s in range(2):
        total = got_ref[s]
        for k in range(s + 2, N, 2):
            total += got_ref[k]
        out_ref[tile(s, s), :] = f_ref[tile(s, s), :] + total[TB : 2 * TB].T
        out_ref[tile(2, s), :] = masked(s, 2, -total[:TB].T)
        out_ref[tile(3, s), :] = masked(s, 3, y[s])
        parts.append(total[2 * TB :])
    out_ref[tile(2, 2), :] = f_ref[tile(2, 2), :] + rows(*parts).T
    out_ref[tile(3, 2), :] = masked(2, 3, -q)
    out_ref[tile(3, 3), :] = f_ref[tile(3, 3), :]


def swap_cores(x):
    return lax.ppermute(x, "col", CORE_SWAP)


def gather_layers(x, begin, ties):
    mine = {0: x}
    other = {}
    late = [0]
    up = down = x
    tied = []
    last = LAYERS // 2
    half = TB // 2
    beside = None
    for step in range(1, last + 1):
        swapped = [swap_cores(mine[d]) for d in late]
        if step == begin[0]:
            swapped, operand = lax.optimization_barrier((swapped, begin[1]))
            beside = begin[2](operand)
        if step == last:
            up, down = up[:, :half], down[:, half:]
        up = lax.ppermute(up, "col", LAYER_UP)
        down = lax.ppermute(down, "col", LAYER_DOWN)
        up, down, swapped, more = lax.optimization_barrier((up, down, swapped, ties.get(step)))
        tied.append(more)
        if step == begin[3]:
            up, down, beside = lax.optimization_barrier((up, down, beside))
        other.update(zip(late, swapped))
        if step < last:
            mine[LAYERS - step], mine[step] = up, down
            late = [LAYERS - step, step]
    mine[last] = jnp.concatenate([up, down], axis=1)
    other[last], beside = lax.optimization_barrier((swap_cores(mine[last]), beside))
    order = range(LAYERS)
    return [mine[d] for d in order], [other[d] for d in order], beside, *(t for t in tied if t is not None)


def body(factor, structure):
    row = lax.axis_index("row")
    col = lax.axis_index("col")
    place = jnp.stack([col, row]).astype(jnp.int32)
    mask = structure.reshape(4, 4, N)
    mask = lax.dynamic_index_in_dim(mask, row, axis=2, keepdims=False)
    flat = factor.reshape(N * TB, TB)
    square = (TB, TB)

    def to_rows(x):
        return lax.all_to_all(x, "row", 0, 0, tiled=True)

    def to_side(x):
        return lax.all_to_all(x, "row", 0, 0, tiled=True, axis_index_groups=SAME_SIDE)

    with jax.named_scope("prepare"):
        l32, away, home, send = call(
            prepare_kernel,
            [square, (4, *square), (4, *square), (N, TB + HALF, TB)],
            mask,
            place,
            flat,
            scalars=2,
        )
    with jax.named_scope("swap_l32"):
        l32_away = lax.ppermute(l32, "row", ROW_SWAP)
        even = lax.rem(row, 2) == 0
        l32_pair = jnp.stack([jnp.where(even, l32, l32_away), jnp.where(even, l32_away, l32)])
    with jax.named_scope("swap_rest"):
        l32_pair, away = lax.optimization_barrier((l32_pair, away))
        away = lax.ppermute(away, "row", ROW_SWAP)
    with jax.named_scope("gather_l"):
        l_mine, l_other, cols, away = gather_layers(
            l32_pair, (1, (send, away), lambda x: to_rows(x[0]), 4), {2: away}
        )
    with jax.named_scope("pack"):
        packed, l3 = call(pack_kernel, [(3, 2, *square), (2, *square)], place, home, away)
    with jax.named_scope("gather_rows"):
        panels = lax.all_gather(packed, "col", axis=0)
        panels = [panels[:, i] for i in range(3)]
        root_rows, diag_rows, l2_rows = panels
    with jax.named_scope("term_t"):
        t, send, l32_rows = call(
            t_kernel,
            [(2, *square), (N // 2, 2, *square), (LAYERS, 2 * TB, 2 * TB)],
            place,
            *l_mine,
            *l_other,
            cols,
            l3,
        )
    with jax.named_scope("term_uq"):
        u, q, q_home, q_away = call(
            uq_kernel,
            [(2, *square), (HALF, 2 * TB), (HALF, TB), (HALF, TB)],
            place,
            root_rows,
            diag_rows,
            cols,
        )
    with jax.named_scope("gather_t"):
        t_mine, t_other, t_cols, (root_rows, l2_rows), (u, q) = gather_layers(
            t, (1, send, to_side, 5), {3: (root_rows, l2_rows), 4: (u, q)}
        )
    with jax.named_scope("term_y"):
        y, y_home, y_away = call(
            y_kernel, [(2 * TB, TB), square, square], place, root_rows, t_cols
        )
    with jax.named_scope("swap_yq"):
        away = jnp.concatenate([y_away, q_away])
        away = lax.ppermute(away, "row", ROW_SWAP)
        y_away, q_away = away[:TB], away[TB:]
    with jax.named_scope("sums"):
        (sums,) = call(
            sums_kernel,
            [(N, 2 * TB + HALF, TB)],
            place,
            *t_mine,
            *t_other,
            l32_rows,
            y,
            u,
            q,
            l2_rows,
        )
    with jax.named_scope("scatter_sums"):
        sums, y_away, q_away = lax.optimization_barrier((sums, y_away, q_away))
        got = lax.all_to_all(sums, "row", 0, 0, tiled=True)
    with jax.named_scope("finish"):
        (out,) = call(
            finish_kernel,
            [(N * TB, TB)],
            mask,
            place,
            flat,
            got,
            y_home,
            y_away,
            q_home,
            q_away,
            scalars=2,
        )
        return out.reshape(factor.shape)


def solution(mesh):
    return jax.shard_map(
        body,
        mesh=mesh,
        in_specs=(P(None, "row", None, "col"), P()),
        out_specs=P(None, "row", None, "col"),
        check_vma=False,
    )
```

```python
import jax
import jax.numpy as jnp
from jax import lax
from jax.experimental import pallas as pl
from jax.experimental.pallas import tpu as pltpu
from jax.sharding import PartitionSpec as P

N = 16
LAYERS = 8
TB = 128
HALF = 64
F32 = jnp.float32
BF16 = jnp.bfloat16
CORE_SWAP = [(i, i ^ 1) for i in range(N)]
ROW_SWAP = [(i, i ^ 1) for i in range(N)]
SAME_SIDE = [[p + 2 * i for i in range(N // 2)] for p in range(2)]
LAYER_UP = [(i, (i + 2) % N) for i in range(N)]
LAYER_DOWN = [(i, (i - 2) % N) for i in range(N)]


def split(x):
    high = x.astype(BF16)
    return high, (x - high.astype(F32)).astype(BF16)


def dot3(a, b):
    a_high, a_low = a
    b_high, b_low = b

    def one(x, y):
        return jnp.dot(x, y, preferred_element_type=F32)

    return one(a_high, b_high) + (one(a_high, b_low) + one(a_low, b_high))


def lanes(*tiles):
    return jnp.concatenate(tiles, axis=1)


def rows(*tiles):
    return jnp.concatenate(tiles, axis=0)


def tile(r, c):
    return pl.ds(r * 4 * TB + c, TB, stride=4)


def call(kernel, shapes, *args, scalars=1):
    smem = pl.BlockSpec(memory_space=pltpu.SMEM)
    vmem = pl.BlockSpec(memory_space=pltpu.VMEM)
    return pl.pallas_call(
        kernel,
        out_shape=[jax.ShapeDtypeStruct(s, F32) for s in shapes],
        in_specs=[smem] * scalars + [vmem] * (len(args) - scalars),
        out_specs=[vmem] * len(shapes),
        compiler_params=pltpu.CompilerParams(vmem_limit_bytes=5 * 2**20),
    )(*args)


def prepare_kernel(mask_ref, place_ref, f_ref, l32_ref, away_ref, home_ref, send_ref):
    side = lax.rem(place_ref[1], 2)

    def lower(r, c):
        return jnp.where(mask_ref[c, r] == 1, f_ref[tile(r, c), :], 0.0)

    x = lower(3, 2)
    l32_ref[...] = x
    turned = x.T
    l2 = [lower(2, s) for s in range(2)]
    l3 = [lower(3, s) for s in range(2)]
    for k in range(N):
        send_ref[k, :TB] = l2[k % 2]
        send_ref[k, TB:] = turned[k % 2 * HALF : (k % 2 + 1) * HALF]
    root, diag = f_ref[tile(3, 3), :], f_ref[tile(2, 2), :]
    away_ref[0] = home_ref[0] = root
    away_ref[1] = home_ref[1] = diag
    even = side == 0
    home_ref[2] = jnp.where(even, l2[0], l2[1])
    away_ref[2] = jnp.where(even, l2[1], l2[0])
    home_ref[3] = jnp.where(even, l3[0], l3[1])
    away_ref[3] = jnp.where(even, l3[1], l3[0])


def pack_kernel(place_ref, home_ref, got_ref, packed_ref, l3_ref):
    side = lax.rem(place_ref[1], 2)
    for i in range(3):
        packed_ref[i, side] = home_ref[i]
        packed_ref[i, 1 - side] = got_ref[i]
    l3_ref[side] = home_ref[3]
    l3_ref[1 - side] = got_ref[3]


def places(place_ref, d):
    layer, core = place_ref[0] // 2, lax.rem(place_ref[0], 2)
    k = lax.rem(layer + d, LAYERS) * 2
    return k + core, k + 1 - core


def t_kernel(place_ref, *refs):
    mine, other = refs[:LAYERS], refs[LAYERS : 2 * LAYERS]
    l2_ref, l3_ref, t_ref, send_ref, all_ref = refs[2 * LAYERS :]
    total = jnp.zeros((2 * TB, TB), F32)
    for d in range(LAYERS):
        k0, k1 = places(place_ref, d)
        a = rows(*(lanes(mine[d][i], other[d][i]) for i in range(2)))
        all_ref[d] = a
        total += dot3(split(a), split(rows(l2_ref[k0, :TB], l2_ref[k1, :TB])))
    for i in range(2):
        x = total[i * TB : (i + 1) * TB] - l3_ref[i]
        t_ref[i] = x
        for k in range(N // 2):
            send_ref[k, i] = x


def pair_rows(rows_ref, k):
    return rows(*(lanes(rows_ref[k, j], rows_ref[k + 1, j]) for j in range(2)))


def dot3_turned(a, b):
    def one(x, y):
        return lax.dot_general(x, y, (((1,), (1,)), ((), ())), preferred_element_type=F32)

    return one(a[0], b[0]) + (one(a[0], b[1]) + one(a[1], b[0]))


def uq_kernel(place_ref, root_ref, diag_ref, cols_ref, u_ref, q_ref, home_ref, away_ref):
    u = jnp.zeros((2 * TB, TB), F32)
    q = jnp.zeros((HALF, 2 * TB), F32)
    for k in range(0, N, 2):
        b = split(rows(cols_ref[k, :TB], cols_ref[k + 1, :TB]))
        u += dot3(split(pair_rows(diag_ref, k)), b)
        b = split(lanes(cols_ref[k, TB:], cols_ref[k + 1, TB:]))
        q += dot3_turned(b, split(pair_rows(root_ref, k)))
    for i in range(2):
        u_ref[i] = u[i * TB : (i + 1) * TB]
    q_ref[...] = q
    even = lax.rem(place_ref[1], 2) == 0
    home_ref[...] = jnp.where(even, q[:, :TB], q[:, TB:])
    away_ref[...] = jnp.where(even, q[:, TB:], q[:, :TB])


def y_kernel(place_ref, root_ref, t_ref, y_ref, home_ref, away_ref):
    y = jnp.zeros((2 * TB, TB), F32)
    for k in range(0, N, 2):
        b = split(rows(t_ref[k // 2, 0], t_ref[k // 2, 1]))
        y += dot3(split(pair_rows(root_ref, k)), b)
    y_ref[...] = y
    even = lax.rem(place_ref[1], 2) == 0
    home_ref[...] = jnp.where(even, y[:TB], y[TB:])
    away_ref[...] = jnp.where(even, y[TB:], y[:TB])


def sums_kernel(place_ref, *refs):
    t_mine, t_other = refs[:LAYERS], refs[LAYERS : 2 * LAYERS]
    l32_ref, y_ref, u_ref, q_ref, l2_ref, sum_ref = refs[2 * LAYERS :]
    row = place_ref[1]
    side = lax.rem(row, 2)
    y = y_ref[...].T
    u = [u_ref[i].T for i in range(2)]
    left = split(rows(y, q_ref[...]))
    yu_split = split(lanes(y, *u))
    for d in range(LAYERS):
        ks = places(place_ref, d)
        low = [lanes(t_mine[d][i], t_other[d][i]) for i in range(2)]
        low += [lanes(l2_ref[ks[0], i], l2_ref[ks[1], i]) for i in range(2)]
        x = dot3(left, split(l32_ref[d]))
        z = dot3(yu_split, split(rows(*low)))
        for i, k in enumerate(ks):
            at = slice(i * TB, (i + 1) * TB)
            sum_ref[k, :TB] = x[:TB, at]
            sum_ref[k, TB : 2 * TB] = z[:, at]
            sum_ref[k, 2 * TB :] = x[TB:, at]
    for i in range(2):
        sum_ref[row - side + i, :TB] += u[i]


def finish_kernel(
    mask_ref, place_ref, f_ref, got_ref, home_ref, away_ref, q_home_ref, q_away_ref, out_ref
):
    even = lax.rem(place_ref[1], 2) == 0

    def masked(s, r, x):
        return jnp.where(mask_ref[s, r] == 1, x, 0.0)

    def both(home, away):
        return [jnp.where(even, home, away), jnp.where(even, away, home)]

    empty = jnp.zeros((TB, TB), F32)
    for r, c in ((0, 1), (0, 2), (0, 3), (1, 0), (1, 2), (1, 3), (2, 3)):
        out_ref[tile(r, c), :] = empty
    y = both(home_ref[...], away_ref[...])
    q = rows(*both(q_home_ref[...], q_away_ref[...])).T
    parts = []
    for s in range(2):
        total = got_ref[s]
        for k in range(s + 2, N, 2):
            total += got_ref[k]
        out_ref[tile(s, s), :] = f_ref[tile(s, s), :] + total[TB : 2 * TB].T
        out_ref[tile(2, s), :] = masked(s, 2, -total[:TB].T)
        out_ref[tile(3, s), :] = masked(s, 3, y[s])
        parts.append(total[2 * TB :])
    out_ref[tile(2, 2), :] = f_ref[tile(2, 2), :] + rows(*parts).T
    out_ref[tile(3, 2), :] = masked(2, 3, -q)
    out_ref[tile(3, 3), :] = f_ref[tile(3, 3), :]


def swap_cores(x):
    return lax.ppermute(x, "col", CORE_SWAP)


def gather_layers(x, begin, ties):
    mine = {0: x}
    other = {}
    late = [0]
    up = down = x
    tied = []
    last = LAYERS // 2
    half = TB // 2
    beside = None
    for step in range(1, last + 1):
        swapped = [swap_cores(mine[d]) for d in late]
        if step == begin[0]:
            swapped, operand = lax.optimization_barrier((swapped, begin[1]))
            beside = begin[2](operand)
        if step == last:
            up, down = up[:, :half], down[:, half:]
        up = lax.ppermute(up, "col", LAYER_UP)
        down = lax.ppermute(down, "col", LAYER_DOWN)
        more = ties.get(step)
        if callable(more):
            more = more(tied[-1])
        up, down, swapped, more = lax.optimization_barrier((up, down, swapped, more))
        tied.append(more)
        if step == begin[3]:
            up, down, beside = lax.optimization_barrier((up, down, beside))
        other.update(zip(late, swapped))
        if step < last:
            mine[LAYERS - step], mine[step] = up, down
            late = [LAYERS - step, step]
    mine[last] = jnp.concatenate([up, down], axis=1)
    other[last], beside = lax.optimization_barrier((swap_cores(mine[last]), beside))
    order = range(LAYERS)
    return [mine[d] for d in order], [other[d] for d in order], beside, *(t for t in tied if t is not None)


def body(factor, structure):
    row = lax.axis_index("row")
    col = lax.axis_index("col")
    place = jnp.stack([col, row]).astype(jnp.int32)
    mask = structure.reshape(4, 4, N)
    mask = lax.dynamic_index_in_dim(mask, row, axis=2, keepdims=False)
    flat = factor.reshape(N * TB, TB)
    square = (TB, TB)

    def to_rows(x):
        return lax.all_to_all(x, "row", 0, 0, tiled=True)

    def to_side(x):
        return lax.all_to_all(x, "row", 0, 0, tiled=True, axis_index_groups=SAME_SIDE)

    with jax.named_scope("prepare"):
        l32, away, home, send = call(
            prepare_kernel,
            [square, (4, *square), (4, *square), (N, TB + HALF, TB)],
            mask,
            place,
            flat,
            scalars=2,
        )
    with jax.named_scope("swap_l32"):
        l32_away = lax.ppermute(l32, "row", ROW_SWAP)
        even = lax.rem(row, 2) == 0
        l32_pair = jnp.stack([jnp.where(even, l32, l32_away), jnp.where(even, l32_away, l32)])
    with jax.named_scope("swap_rest"):
        l32_pair, away = lax.optimization_barrier((l32_pair, away))
        away = lax.ppermute(away, "row", ROW_SWAP)
    def pack(away):
        return call(pack_kernel, [(3, 2, *square), (2, *square)], place, home, away)

    with jax.named_scope("gather_l"):
        l_mine, l_other, cols, _, (packed, l3) = gather_layers(
            l32_pair, (2, (send, away), lambda x: to_rows(x[0]), 4), {1: away, 2: pack}
        )
    with jax.named_scope("gather_rows"):
        panels = lax.all_gather(packed, "col", axis=0)
        panels = [panels[:, i] for i in range(3)]
        root_rows, diag_rows, l2_rows = panels
    with jax.named_scope("term_t"):
        t, send, l32_rows = call(
            t_kernel,
            [(2, *square), (N // 2, 2, *square), (LAYERS, 2 * TB, 2 * TB)],
            place,
            *l_mine,
            *l_other,
            cols,
            l3,
        )
    with jax.named_scope("term_uq"):
        u, q, q_home, q_away = call(
            uq_kernel,
            [(2, *square), (HALF, 2 * TB), (HALF, TB), (HALF, TB)],
            place,
            root_rows,
            diag_rows,
            cols,
        )
    with jax.named_scope("gather_t"):
        t_mine, t_other, t_cols, (root_rows, l2_rows), (u, q) = gather_layers(
            t, (1, send, to_side, 5), {3: (root_rows, l2_rows), 4: (u, q)}
        )
    with jax.named_scope("term_y"):
        y, y_home, y_away = call(
            y_kernel, [(2 * TB, TB), square, square], place, root_rows, t_cols
        )
    with jax.named_scope("swap_yq"):
        away = jnp.concatenate([y_away, q_away])
        away = lax.ppermute(away, "row", ROW_SWAP)
        y_away, q_away = away[:TB], away[TB:]
    with jax.named_scope("sums"):
        (sums,) = call(
            sums_kernel,
            [(N, 2 * TB + HALF, TB)],
            place,
            *t_mine,
            *t_other,
            l32_rows,
            y,
            u,
            q,
            l2_rows,
        )
    with jax.named_scope("scatter_sums"):
        sums, y_away, q_away = lax.optimization_barrier((sums, y_away, q_away))
        got = lax.all_to_all(sums, "row", 0, 0, tiled=True)
    with jax.named_scope("finish"):
        (out,) = call(
            finish_kernel,
            [(N * TB, TB)],
            mask,
            place,
            flat,
            got,
            y_home,
            y_away,
            q_home,
            q_away,
            scalars=2,
        )
        return out.reshape(factor.shape)


def solution(mesh):
    return jax.shard_map(
        body,
        mesh=mesh,
        in_specs=(P(None, "row", None, "col"), P()),
        out_specs=P(None, "row", None, "col"),
        check_vma=False,
    )
```

```python
import jax
import jax.numpy as jnp
from jax import lax
from jax.experimental import pallas as pl
from jax.experimental.pallas import tpu as pltpu
from jax.sharding import PartitionSpec as P

N = 16
LAYERS = 8
TILES = LAYERS + 1
TB = 128
HALF = 64
F32 = jnp.float32
BF16 = jnp.bfloat16
CORE_SWAP = [(i, i ^ 1) for i in range(N)]
ROW_SWAP = [(i, i ^ 1) for i in range(N)]
SAME_SIDE = [[p + 2 * i for i in range(N // 2)] for p in range(2)]
LAYER_UP = [(i, (i + 2) % N) for i in range(N)]
LAYER_DOWN = [(i, (i - 2) % N) for i in range(N)]


def split(x):
    high = x.astype(BF16)
    return high, (x - high.astype(F32)).astype(BF16)


def dot3(a, b):
    a_high, a_low = a
    b_high, b_low = b

    def one(x, y):
        return jnp.dot(x, y, preferred_element_type=F32)

    return one(a_high, b_high) + (one(a_high, b_low) + one(a_low, b_high))


def lanes(*tiles):
    return jnp.concatenate(tiles, axis=1)


def rows(*tiles):
    return jnp.concatenate(tiles, axis=0)


def tile(r, c):
    return pl.ds(r * 4 * TB + c, TB, stride=4)


def call(kernel, shapes, *args, scalars=1):
    smem = pl.BlockSpec(memory_space=pltpu.SMEM)
    vmem = pl.BlockSpec(memory_space=pltpu.VMEM)
    return pl.pallas_call(
        kernel,
        out_shape=[jax.ShapeDtypeStruct(s, F32) for s in shapes],
        in_specs=[smem] * scalars + [vmem] * (len(args) - scalars),
        out_specs=[vmem] * len(shapes),
        compiler_params=pltpu.CompilerParams(vmem_limit_bytes=5 * 2**20),
    )(*args)


def prepare_kernel(mask_ref, place_ref, f_ref, l32_ref, away_ref, home_ref, send_ref):
    side = lax.rem(place_ref[1], 2)

    def lower(r, c):
        return jnp.where(mask_ref[c, r] == 1, f_ref[tile(r, c), :], 0.0)

    x = lower(3, 2)
    l32_ref[...] = x
    turned = x.T
    l2 = [lower(2, s) for s in range(2)]
    l3 = [lower(3, s) for s in range(2)]
    for k in range(N):
        send_ref[k, :TB] = l2[k % 2]
        send_ref[k, TB:] = turned[k % 2 * HALF : (k % 2 + 1) * HALF]
    root, diag = f_ref[tile(3, 3), :], f_ref[tile(2, 2), :]
    away_ref[0] = home_ref[0] = root
    away_ref[1] = home_ref[1] = diag
    even = side == 0
    home_ref[2] = jnp.where(even, l2[0], l2[1])
    away_ref[2] = jnp.where(even, l2[1], l2[0])
    home_ref[3] = jnp.where(even, l3[0], l3[1])
    away_ref[3] = jnp.where(even, l3[1], l3[0])


def pack_kernel(place_ref, home_ref, got_ref, packed_ref, l3_ref):
    side = lax.rem(place_ref[1], 2)
    for i in range(3):
        packed_ref[i, side] = home_ref[i]
        packed_ref[i, 1 - side] = got_ref[i]
    l3_ref[side] = home_ref[3]
    l3_ref[1 - side] = got_ref[3]


def places(place_ref, d):
    layer, core = place_ref[0] // 2, lax.rem(place_ref[0], 2)
    k = lax.rem(layer + d, LAYERS) * 2
    return k + core, k + 1 - core


def tiles_at(refs, d):
    last = LAYERS // 2
    if d == last:
        return refs[last][0], refs[last + 1][0]
    ref = refs[d + (d > last)]
    return ref[0], ref[1]


def both_cores(mine, other, d):
    return [lanes(*pair) for pair in zip(tiles_at(mine, d), tiles_at(other, d))]


def t_kernel(place_ref, *refs):
    mine, other = refs[:TILES], refs[TILES : 2 * TILES]
    l2_ref, l3_ref, t_ref, send_ref, all_ref = refs[2 * TILES :]
    total = jnp.zeros((2 * TB, TB), F32)
    for d in range(LAYERS):
        k0, k1 = places(place_ref, d)
        a = rows(*both_cores(mine, other, d))
        all_ref[d] = a
        total += dot3(split(a), split(rows(l2_ref[k0, :TB], l2_ref[k1, :TB])))
    for i in range(2):
        x = total[i * TB : (i + 1) * TB] - l3_ref[i]
        t_ref[i] = x
        for k in range(N // 2):
            send_ref[k, i] = x


def pair_rows(rows_ref, k):
    return rows(*(lanes(rows_ref[k, j], rows_ref[k + 1, j]) for j in range(2)))


def dot3_turned(a, b):
    def one(x, y):
        return lax.dot_general(x, y, (((1,), (1,)), ((), ())), preferred_element_type=F32)

    return one(a[0], b[0]) + (one(a[0], b[1]) + one(a[1], b[0]))


def uq_kernel(root_ref, diag_ref, cols_ref, u_ref, q_ref):
    u = jnp.zeros((2 * TB, TB), F32)
    q = jnp.zeros((HALF, 2 * TB), F32)
    for k in range(0, N, 2):
        b = split(rows(cols_ref[k, :TB], cols_ref[k + 1, :TB]))
        u += dot3(split(pair_rows(diag_ref, k)), b)
        b = split(lanes(cols_ref[k, TB:], cols_ref[k + 1, TB:]))
        q += dot3_turned(b, split(pair_rows(root_ref, k)))
    for i in range(2):
        u_ref[i] = u[i * TB : (i + 1) * TB]
    q_ref[...] = q


def y_kernel(place_ref, root_ref, t_ref, y_ref, home_ref, away_ref):
    y = jnp.zeros((2 * TB, TB), F32)
    for k in range(0, N, 2):
        b = split(rows(t_ref[k // 2, 0], t_ref[k // 2, 1]))
        y += dot3(split(pair_rows(root_ref, k)), b)
    y_ref[...] = y
    even = lax.rem(place_ref[1], 2) == 0
    home_ref[...] = jnp.where(even, y[:TB], y[TB:])
    away_ref[...] = jnp.where(even, y[TB:], y[:TB])


def sums_kernel(place_ref, *refs):
    t_mine, t_other = refs[:TILES], refs[TILES : 2 * TILES]
    l32_ref, y_ref, u_ref, q_ref, l2_ref, sum_ref = refs[2 * TILES :]
    row = place_ref[1]
    side = lax.rem(row, 2)
    y = y_ref[...].T
    u = [u_ref[i].T for i in range(2)]
    left = split(rows(y, q_ref[...]))
    yu_split = split(lanes(y, *u))
    for d in range(LAYERS):
        ks = places(place_ref, d)
        low = both_cores(t_mine, t_other, d)
        low += [lanes(l2_ref[ks[0], i], l2_ref[ks[1], i]) for i in range(2)]
        x = dot3(left, split(l32_ref[d]))
        z = dot3(yu_split, split(rows(*low)))
        for i, k in enumerate(ks):
            at = slice(i * TB, (i + 1) * TB)
            sum_ref[k, :TB] = x[:TB, at]
            sum_ref[k, TB : 2 * TB] = z[:, at]
            sum_ref[k, 2 * TB :] = x[TB:, at]
    for i in range(2):
        sum_ref[row - side + i, :TB] += u[i]


def finish_kernel(
    mask_ref, place_ref, f_ref, got_ref, home_ref, away_ref, q_home_ref, q_away_ref, out_ref
):
    even = lax.rem(place_ref[1], 2) == 0

    def masked(s, r, x):
        return jnp.where(mask_ref[s, r] == 1, x, 0.0)

    def both(home, away):
        return [jnp.where(even, home, away), jnp.where(even, away, home)]

    empty = jnp.zeros((TB, TB), F32)
    for r, c in ((0, 1), (0, 2), (0, 3), (1, 0), (1, 2), (1, 3), (2, 3)):
        out_ref[tile(r, c), :] = empty
    y = both(home_ref[...], away_ref[...])
    q = rows(*both(q_home_ref[...], q_away_ref[...]))
    q = jnp.where(even, q[:, :TB], q[:, TB:]).T
    parts = []
    for s in range(2):
        total = got_ref[s]
        for k in range(s + 2, N, 2):
            total += got_ref[k]
        out_ref[tile(s, s), :] = f_ref[tile(s, s), :] + total[TB : 2 * TB].T
        out_ref[tile(2, s), :] = masked(s, 2, -total[:TB].T)
        out_ref[tile(3, s), :] = masked(s, 3, y[s])
        parts.append(total[2 * TB :])
    out_ref[tile(2, 2), :] = f_ref[tile(2, 2), :] + rows(*parts).T
    out_ref[tile(3, 2), :] = masked(2, 3, -q)
    out_ref[tile(3, 3), :] = f_ref[tile(3, 3), :]


def swap_cores(x):
    return lax.ppermute(x, "col", CORE_SWAP)


def gather_layers(x, begin, ties):
    mine = {0: x}
    other = {}
    late = [0]
    up = down = x
    tied = []
    last = LAYERS // 2
    beside = None
    for step in range(1, last + 1):
        swapped = [swap_cores(mine[d]) for d in late]
        if step == begin[0]:
            swapped, operand = lax.optimization_barrier((swapped, begin[1]))
            beside = begin[2](operand)
        if step == last:
            up, down = up[:1], down[1:]
        up = lax.ppermute(up, "col", LAYER_UP)
        down = lax.ppermute(down, "col", LAYER_DOWN)
        more = ties.get(step)
        if callable(more):
            more = more(tied[-1])
        up, down, swapped, more = lax.optimization_barrier((up, down, swapped, more))
        tied.append(more)
        if step == begin[3]:
            up, down, beside = lax.optimization_barrier((up, down, beside))
        other.update(zip(late, swapped))
        if step < last:
            mine[LAYERS - step], mine[step] = up, down
            late = [LAYERS - step, step]
    swapped, beside = lax.optimization_barrier(([swap_cores(up), swap_cores(down)], beside))
    near, far = range(last), range(last + 1, LAYERS)
    mine = [*(mine[d] for d in near), up, down, *(mine[d] for d in far)]
    other = [*(other[d] for d in near), *swapped, *(other[d] for d in far)]
    return mine, other, beside, *(t for t in tied if t is not None)


def body(factor, structure):
    row = lax.axis_index("row")
    col = lax.axis_index("col")
    place = jnp.stack([col, row]).astype(jnp.int32)
    mask = structure.reshape(4, 4, N)
    mask = lax.dynamic_index_in_dim(mask, row, axis=2, keepdims=False)
    flat = factor.reshape(N * TB, TB)
    square = (TB, TB)

    def to_rows(x):
        return lax.all_to_all(x, "row", 0, 0, tiled=True)

    def to_side(x):
        return lax.all_to_all(x, "row", 0, 0, tiled=True, axis_index_groups=SAME_SIDE)

    with jax.named_scope("prepare"):
        l32, away, home, send = call(
            prepare_kernel,
            [square, (4, *square), (4, *square), (N, TB + HALF, TB)],
            mask,
            place,
            flat,
            scalars=2,
        )
    with jax.named_scope("swap_l32"):
        l32_away = lax.ppermute(l32, "row", ROW_SWAP)
        even = lax.rem(row, 2) == 0
        l32_pair = jnp.stack([jnp.where(even, l32, l32_away), jnp.where(even, l32_away, l32)])
    with jax.named_scope("swap_rest"):
        l32_pair, away = lax.optimization_barrier((l32_pair, away))
        away = lax.ppermute(away, "row", ROW_SWAP)
    def pack(away):
        return call(pack_kernel, [(3, 2, *square), (2, *square)], place, home, away)

    with jax.named_scope("gather_l"):
        l_mine, l_other, cols, _, (packed, l3) = gather_layers(
            l32_pair, (2, (send, away), lambda x: to_rows(x[0]), 4), {1: away, 2: pack}
        )
    with jax.named_scope("gather_rows"):
        panels = lax.all_gather(packed, "col", axis=0)
        panels = [panels[:, i] for i in range(3)]
        root_rows, diag_rows, l2_rows = panels
    with jax.named_scope("term_t"):
        t, send, l32_rows = call(
            t_kernel,
            [(2, *square), (N // 2, 2, *square), (LAYERS, 2 * TB, 2 * TB)],
            place,
            *l_mine,
            *l_other,
            cols,
            l3,
        )
    with jax.named_scope("term_uq"):
        u, q = call(
            uq_kernel,
            [(2, *square), (HALF, 2 * TB)],
            root_rows,
            diag_rows,
            cols,
            scalars=0,
        )
    with jax.named_scope("gather_t"):
        t_mine, t_other, t_cols, (root_rows, l2_rows), (u, q) = gather_layers(
            t, (1, send, to_side, 5), {3: (root_rows, l2_rows), 4: (u, q)}
        )
    with jax.named_scope("term_y"):
        y, y_home, y_away = call(
            y_kernel, [(2 * TB, TB), square, square], place, root_rows, t_cols
        )
    with jax.named_scope("swap_yq"):
        y_away = lax.ppermute(y_away, "row", ROW_SWAP)
        q_away = lax.ppermute(q, "row", ROW_SWAP)
    with jax.named_scope("sums"):
        (sums,) = call(
            sums_kernel,
            [(N, 2 * TB + HALF, TB)],
            place,
            *t_mine,
            *t_other,
            l32_rows,
            y,
            u,
            q,
            l2_rows,
        )
    with jax.named_scope("scatter_sums"):
        sums, y_away, q_away = lax.optimization_barrier((sums, y_away, q_away))
        got = lax.all_to_all(sums, "row", 0, 0, tiled=True)
    with jax.named_scope("finish"):
        (out,) = call(
            finish_kernel,
            [(N * TB, TB)],
            mask,
            place,
            flat,
            got,
            y_home,
            y_away,
            q,
            q_away,
            scalars=2,
        )
        return out.reshape(factor.shape)


def solution(mesh):
    return jax.shard_map(
        body,
        mesh=mesh,
        in_specs=(P(None, "row", None, "col"), P()),
        out_specs=P(None, "row", None, "col"),
        check_vma=False,
    )
```

```python
import jax
import jax.numpy as jnp
from jax import lax
from jax.experimental import pallas as pl
from jax.experimental.pallas import tpu as pltpu
from jax.sharding import PartitionSpec as P

N = 16
LAYERS = 8
TILES = LAYERS + 1
TB = 128
HALF = 64
F32 = jnp.float32
BF16 = jnp.bfloat16
CORE_SWAP = [(i, i ^ 1) for i in range(N)]
ROW_SWAP = [(i, i ^ 1) for i in range(N)]
SAME_SIDE = [[p + 2 * i for i in range(N // 2)] for p in range(2)]


def split(x):
    high = x.astype(BF16)
    return high, (x - high.astype(F32)).astype(BF16)


def dot3(a, b):
    a_high, a_low = a
    b_high, b_low = b

    def one(x, y):
        return jnp.dot(x, y, preferred_element_type=F32)

    return one(a_high, b_high) + (one(a_high, b_low) + one(a_low, b_high))


def lanes(*tiles):
    return jnp.concatenate(tiles, axis=1)


def rows(*tiles):
    return jnp.concatenate(tiles, axis=0)


def tile(r, c):
    return pl.ds(r * 4 * TB + c, TB, stride=4)


def call(kernel, shapes, *args, scalars=1):
    smem = pl.BlockSpec(memory_space=pltpu.SMEM)
    vmem = pl.BlockSpec(memory_space=pltpu.VMEM)
    return pl.pallas_call(
        kernel,
        out_shape=[jax.ShapeDtypeStruct(s, F32) for s in shapes],
        in_specs=[smem] * scalars + [vmem] * (len(args) - scalars),
        out_specs=[vmem] * len(shapes),
        compiler_params=pltpu.CompilerParams(vmem_limit_bytes=5 * 2**20),
    )(*args)


def prepare_kernel(mask_ref, place_ref, f_ref, l32_ref, away_ref, home_ref, send_ref):
    side = lax.rem(place_ref[1], 2)

    def lower(r, c):
        return jnp.where(mask_ref[c, r] == 1, f_ref[tile(r, c), :], 0.0)

    x = lower(3, 2)
    l32_ref[...] = x
    turned = x.T
    l2 = [lower(2, s) for s in range(2)]
    l3 = [lower(3, s) for s in range(2)]
    for k in range(N):
        send_ref[k, :TB] = l2[k % 2]
        send_ref[k, TB:] = turned[k % 2 * HALF : (k % 2 + 1) * HALF]
    root, diag = f_ref[tile(3, 3), :], f_ref[tile(2, 2), :]
    away_ref[0] = home_ref[0] = root
    away_ref[1] = home_ref[1] = diag
    even = side == 0
    home_ref[2] = jnp.where(even, l2[0], l2[1])
    away_ref[2] = jnp.where(even, l2[1], l2[0])
    home_ref[3] = jnp.where(even, l3[0], l3[1])
    away_ref[3] = jnp.where(even, l3[1], l3[0])


def pack_kernel(place_ref, home_ref, got_ref, packed_ref, l3_ref):
    side = lax.rem(place_ref[1], 2)
    for i in range(3):
        packed_ref[i, side] = home_ref[i]
        packed_ref[i, 1 - side] = got_ref[i]
    l3_ref[side] = home_ref[3]
    l3_ref[1 - side] = got_ref[3]


def places(place_ref, d):
    layer, core = place_ref[0] // 2, lax.rem(place_ref[0], 2)
    k = lax.rem(layer + d, LAYERS) * 2
    return k + core, k + 1 - core


def tiles_at(refs, d):
    last = LAYERS // 2
    if d == last:
        return refs[last][0], refs[last + 1][0]
    ref = refs[d + (d > last)]
    return ref[0], ref[1]


def both_cores(mine, other, d):
    return [lanes(*pair) for pair in zip(tiles_at(mine, d), tiles_at(other, d))]


def t_kernel(place_ref, *refs):
    mine, other = refs[:TILES], refs[TILES : 2 * TILES]
    l2_ref, l3_ref, t_ref, send_ref, all_ref = refs[2 * TILES :]
    total = jnp.zeros((2 * TB, TB), F32)
    for d in range(LAYERS):
        k0, k1 = places(place_ref, d)
        a = rows(*both_cores(mine, other, d))
        all_ref[d] = a
        total += dot3(split(a), split(rows(l2_ref[k0, :TB], l2_ref[k1, :TB])))
    for i in range(2):
        x = total[i * TB : (i + 1) * TB] - l3_ref[i]
        t_ref[i] = x
        for k in range(N // 2):
            send_ref[k, i] = x


def pair_rows(rows_ref, k):
    return rows(*(lanes(rows_ref[k, j], rows_ref[k + 1, j]) for j in range(2)))


def dot3_turned(a, b):
    def one(x, y):
        return lax.dot_general(x, y, (((1,), (1,)), ((), ())), preferred_element_type=F32)

    return one(a[0], b[0]) + (one(a[0], b[1]) + one(a[1], b[0]))


def uq_kernel(root_ref, diag_ref, cols_ref, u_ref, q_ref):
    u = jnp.zeros((2 * TB, TB), F32)
    q = jnp.zeros((HALF, 2 * TB), F32)
    for k in range(0, N, 2):
        b = split(rows(cols_ref[k, :TB], cols_ref[k + 1, :TB]))
        u += dot3(split(pair_rows(diag_ref, k)), b)
        b = split(lanes(cols_ref[k, TB:], cols_ref[k + 1, TB:]))
        q += dot3_turned(b, split(pair_rows(root_ref, k)))
    for i in range(2):
        u_ref[i] = u[i * TB : (i + 1) * TB]
    q_ref[...] = q


def y_kernel(place_ref, root_ref, t_ref, y_ref, home_ref, away_ref):
    y = jnp.zeros((2 * TB, TB), F32)
    for k in range(0, N, 2):
        b = split(rows(t_ref[k // 2, 0], t_ref[k // 2, 1]))
        y += dot3(split(pair_rows(root_ref, k)), b)
    y_ref[...] = y
    even = lax.rem(place_ref[1], 2) == 0
    home_ref[...] = jnp.where(even, y[:TB], y[TB:])
    away_ref[...] = jnp.where(even, y[TB:], y[:TB])


def sums_kernel(place_ref, *refs):
    t_mine, t_other = refs[:TILES], refs[TILES : 2 * TILES]
    l32_ref, y_ref, u_ref, q_ref, l2_ref, sum_ref = refs[2 * TILES :]
    row = place_ref[1]
    side = lax.rem(row, 2)
    y = y_ref[...].T
    u = [u_ref[i].T for i in range(2)]
    left = split(rows(y, q_ref[...]))
    yu_split = split(lanes(y, *u))
    for d in range(LAYERS):
        ks = places(place_ref, d)
        low = both_cores(t_mine, t_other, d)
        low += [lanes(l2_ref[ks[0], i], l2_ref[ks[1], i]) for i in range(2)]
        x = dot3(left, split(l32_ref[d]))
        z = dot3(yu_split, split(rows(*low)))
        for i, k in enumerate(ks):
            at = slice(i * TB, (i + 1) * TB)
            sum_ref[k, :TB] = x[:TB, at]
            sum_ref[k, TB : 2 * TB] = z[:, at]
            sum_ref[k, 2 * TB :] = x[TB:, at]
    for i in range(2):
        sum_ref[row - side + i, :TB] += u[i]


def finish_kernel(
    mask_ref, place_ref, f_ref, got_ref, home_ref, away_ref, q_home_ref, q_away_ref, out_ref
):
    even = lax.rem(place_ref[1], 2) == 0

    def masked(s, r, x):
        return jnp.where(mask_ref[s, r] == 1, x, 0.0)

    def both(home, away):
        return [jnp.where(even, home, away), jnp.where(even, away, home)]

    empty = jnp.zeros((TB, TB), F32)
    for r, c in ((0, 1), (0, 2), (0, 3), (1, 0), (1, 2), (1, 3), (2, 3)):
        out_ref[tile(r, c), :] = empty
    y = both(home_ref[...], away_ref[...])
    q = rows(*both(q_home_ref[...], q_away_ref[...]))
    q = jnp.where(even, q[:, :TB], q[:, TB:]).T
    parts = []
    for s in range(2):
        total = got_ref[s]
        for k in range(s + 2, N, 2):
            total += got_ref[k]
        out_ref[tile(s, s), :] = f_ref[tile(s, s), :] + total[TB : 2 * TB].T
        out_ref[tile(2, s), :] = masked(s, 2, -total[:TB].T)
        out_ref[tile(3, s), :] = masked(s, 3, y[s])
        parts.append(total[2 * TB :])
    out_ref[tile(2, 2), :] = f_ref[tile(2, 2), :] + rows(*parts).T
    out_ref[tile(3, 2), :] = masked(2, 3, -q)
    out_ref[tile(3, 3), :] = f_ref[tile(3, 3), :]


def swap_cores(x):
    return lax.ppermute(x, "col", CORE_SWAP)


def shift(x, layers):
    return lax.ppermute(x, "col", [(i, (i + 2 * layers) % N) for i in range(N)])


def gather_layers(x, begin, ties):
    def tie(values, more, before):
        if callable(more):
            more = more(before)
        return lax.optimization_barrier((values, more))

    near = [shift(x, -1), shift(x, -2), shift(x, 2), shift(x, 1)]
    (near, own), first = tie((near, swap_cores(x)), ties[0], None)
    far = [shift(near[0], -2), shift(near[2][:1], 2), shift(near[1][1:], -2), shift(near[3], 2)]
    beside = begin[1](begin[0])
    (far, near_swapped), second = tie((far, [swap_cores(t) for t in near]), ties[1], first)
    far_swapped, beside = lax.optimization_barrier(([swap_cores(t) for t in far], beside))
    mine = [x, *near[:2], *far, *near[2:]]
    other = [own, *near_swapped[:2], *far_swapped, *near_swapped[2:]]
    return mine, other, beside, first, second


def body(factor, structure):
    row = lax.axis_index("row")
    col = lax.axis_index("col")
    place = jnp.stack([col, row]).astype(jnp.int32)
    mask = structure.reshape(4, 4, N)
    mask = lax.dynamic_index_in_dim(mask, row, axis=2, keepdims=False)
    flat = factor.reshape(N * TB, TB)
    square = (TB, TB)

    def to_rows(x):
        return lax.all_to_all(x, "row", 0, 0, tiled=True)

    def to_side(x):
        return lax.all_to_all(x, "row", 0, 0, tiled=True, axis_index_groups=SAME_SIDE)

    with jax.named_scope("prepare"):
        l32, away, home, send = call(
            prepare_kernel,
            [square, (4, *square), (4, *square), (N, TB + HALF, TB)],
            mask,
            place,
            flat,
            scalars=2,
        )
    with jax.named_scope("swap_l32"):
        l32_away = lax.ppermute(l32, "row", ROW_SWAP)
        even = lax.rem(row, 2) == 0
        l32_pair = jnp.stack([jnp.where(even, l32, l32_away), jnp.where(even, l32_away, l32)])
    with jax.named_scope("swap_rest"):
        l32_pair, away = lax.optimization_barrier((l32_pair, away))
        away = lax.ppermute(away, "row", ROW_SWAP)
    def pack(away):
        return call(pack_kernel, [(3, 2, *square), (2, *square)], place, home, away)

    with jax.named_scope("gather_l"):
        send, away = lax.optimization_barrier((send, away))
        l_mine, l_other, cols, away, _ = gather_layers(l32_pair, (send, to_rows), (away, None))
    with jax.named_scope("pack"):
        packed, l3 = pack(away)
    with jax.named_scope("gather_rows"):
        panels = lax.all_gather(packed, "col", axis=0)
        panels = [panels[:, i] for i in range(3)]
        root_rows, diag_rows, l2_rows = panels
    with jax.named_scope("term_t"):
        t, send, l32_rows = call(
            t_kernel,
            [(2, *square), (N // 2, 2, *square), (LAYERS, 2 * TB, 2 * TB)],
            place,
            *l_mine,
            *l_other,
            cols,
            l3,
        )
    with jax.named_scope("term_uq"):
        u, q = call(
            uq_kernel,
            [(2, *square), (HALF, 2 * TB)],
            root_rows,
            diag_rows,
            cols,
            scalars=0,
        )
    with jax.named_scope("gather_t"):
        t_mine, t_other, t_cols, _, (root_rows, l2_rows, u, q) = gather_layers(
            t, (send, to_side), (None, lambda _: (root_rows, l2_rows, u, q))
        )
    with jax.named_scope("term_y"):
        y, y_home, y_away = call(
            y_kernel, [(2 * TB, TB), square, square], place, root_rows, t_cols
        )
    with jax.named_scope("swap_yq"):
        y_away = lax.ppermute(y_away, "row", ROW_SWAP)
        q_away = lax.ppermute(q, "row", ROW_SWAP)
    with jax.named_scope("sums"):
        (sums,) = call(
            sums_kernel,
            [(N, 2 * TB + HALF, TB)],
            place,
            *t_mine,
            *t_other,
            l32_rows,
            y,
            u,
            q,
            l2_rows,
        )
    with jax.named_scope("scatter_sums"):
        sums, y_away, q_away = lax.optimization_barrier((sums, y_away, q_away))
        got = lax.all_to_all(sums, "row", 0, 0, tiled=True)
    with jax.named_scope("finish"):
        (out,) = call(
            finish_kernel,
            [(N * TB, TB)],
            mask,
            place,
            flat,
            got,
            y_home,
            y_away,
            q,
            q_away,
            scalars=2,
        )
        return out.reshape(factor.shape)


def solution(mesh):
    return jax.shard_map(
        body,
        mesh=mesh,
        in_specs=(P(None, "row", None, "col"), P()),
        out_specs=P(None, "row", None, "col"),
        check_vma=False,
    )
```

```python
import jax
import jax.numpy as jnp
from jax import lax
from jax.experimental import pallas as pl
from jax.experimental.pallas import tpu as pltpu
from jax.sharding import PartitionSpec as P

N = 16
LAYERS = 8
TB = 128
HALF = 64
F32 = jnp.float32
BF16 = jnp.bfloat16
CORE_SWAP = [(i, i ^ 1) for i in range(N)]
ROW_SWAP = [(i, i ^ 1) for i in range(N)]
SAME_SIDE = [[p + 2 * i for i in range(N // 2)] for p in range(2)]
LAYER_UP = [(i, (i + 2) % N) for i in range(N)]
LAYER_DOWN = [(i, (i - 2) % N) for i in range(N)]


def split(x):
    high = x.astype(BF16)
    return high, (x - high.astype(F32)).astype(BF16)


def dot3(a, b):
    a_high, a_low = a
    b_high, b_low = b

    def one(x, y):
        return jnp.dot(x, y, preferred_element_type=F32)

    return one(a_high, b_high) + (one(a_high, b_low) + one(a_low, b_high))


def lanes(*tiles):
    return jnp.concatenate(tiles, axis=1)


def rows(*tiles):
    return jnp.concatenate(tiles, axis=0)


def tile(r, c):
    return pl.ds(r * 4 * TB + c, TB, stride=4)


def call(kernel, shapes, *args, scalars=1):
    smem = pl.BlockSpec(memory_space=pltpu.SMEM)
    vmem = pl.BlockSpec(memory_space=pltpu.VMEM)
    return pl.pallas_call(
        kernel,
        out_shape=[jax.ShapeDtypeStruct(s, F32) for s in shapes],
        in_specs=[smem] * scalars + [vmem] * (len(args) - scalars),
        out_specs=[vmem] * len(shapes),
        compiler_params=pltpu.CompilerParams(vmem_limit_bytes=5 * 2**20),
    )(*args)


def prepare_kernel(mask_ref, place_ref, f_ref, l32_ref, away_ref, home_ref, send_ref):
    side = lax.rem(place_ref[1], 2)

    def lower(r, c):
        return jnp.where(mask_ref[c, r] == 1, f_ref[tile(r, c), :], 0.0)

    x = lower(3, 2)
    l32_ref[...] = x
    turned = x.T
    l2 = [lower(2, s) for s in range(2)]
    l3 = [lower(3, s) for s in range(2)]
    for k in range(N):
        send_ref[k, :TB] = l2[k % 2]
        send_ref[k, TB:] = turned[k % 2 * HALF : (k % 2 + 1) * HALF]
    root, diag = f_ref[tile(3, 3), :], f_ref[tile(2, 2), :]
    away_ref[0] = home_ref[0] = root
    away_ref[1] = home_ref[1] = diag
    even = side == 0
    home_ref[2] = jnp.where(even, l2[0], l2[1])
    away_ref[2] = jnp.where(even, l2[1], l2[0])
    home_ref[3] = jnp.where(even, l3[0], l3[1])
    away_ref[3] = jnp.where(even, l3[1], l3[0])


def pack_kernel(place_ref, home_ref, got_ref, packed_ref, l3_ref):
    side = lax.rem(place_ref[1], 2)
    for i in range(3):
        packed_ref[i, side] = home_ref[i]
        packed_ref[i, 1 - side] = got_ref[i]
    l3_ref[side] = home_ref[3]
    l3_ref[1 - side] = got_ref[3]


def places(place_ref, d):
    layer, core = place_ref[0] // 2, lax.rem(place_ref[0], 2)
    k = lax.rem(layer + d, LAYERS) * 2
    return k + core, k + 1 - core


def t_kernel(place_ref, *refs):
    mine, other = refs[:LAYERS], refs[LAYERS : 2 * LAYERS]
    l2_ref, l3_ref, t_ref, send_ref, all_ref = refs[2 * LAYERS :]
    total = jnp.zeros((2 * TB, TB), F32)
    for d in range(LAYERS):
        k0, k1 = places(place_ref, d)
        a = rows(*(lanes(mine[d][i], other[d][i]) for i in range(2)))
        all_ref[d] = a
        total += dot3(split(a), split(rows(l2_ref[k0, :TB], l2_ref[k1, :TB])))
    for i in range(2):
        x = total[i * TB : (i + 1) * TB] - l3_ref[i]
        t_ref[i] = x
        for k in range(N // 2):
            send_ref[k, i] = x


def pair_rows(rows_ref, k):
    return rows(*(lanes(rows_ref[k, j], rows_ref[k + 1, j]) for j in range(2)))


def dot3_turned(a, b):
    def one(x, y):
        return lax.dot_general(x, y, (((1,), (1,)), ((), ())), preferred_element_type=F32)

    return one(a[0], b[0]) + (one(a[0], b[1]) + one(a[1], b[0]))


def uq_kernel(root_ref, diag_ref, cols_ref, u_ref, q_ref):
    u = jnp.zeros((2 * TB, TB), F32)
    q = jnp.zeros((HALF, 2 * TB), F32)
    for k in range(0, N, 2):
        b = split(rows(cols_ref[k, :TB], cols_ref[k + 1, :TB]))
        u += dot3(split(pair_rows(diag_ref, k)), b)
        b = split(lanes(cols_ref[k, TB:], cols_ref[k + 1, TB:]))
        q += dot3_turned(b, split(pair_rows(root_ref, k)))
    for i in range(2):
        u_ref[i] = u[i * TB : (i + 1) * TB]
    q_ref[...] = q


def y_kernel(place_ref, root_ref, t_ref, y_ref, home_ref, away_ref):
    y = jnp.zeros((2 * TB, TB), F32)
    for k in range(0, N, 2):
        b = split(rows(t_ref[k // 2, 0], t_ref[k // 2, 1]))
        y += dot3(split(pair_rows(root_ref, k)), b)
    y_ref[...] = y
    even = lax.rem(place_ref[1], 2) == 0
    home_ref[...] = jnp.where(even, y[:TB], y[TB:])
    away_ref[...] = jnp.where(even, y[TB:], y[:TB])


def sums_kernel(place_ref, *refs):
    t_mine, t_other = refs[:LAYERS], refs[LAYERS : 2 * LAYERS]
    l32_ref, y_ref, u_ref, q_ref, l2_ref, sum_ref = refs[2 * LAYERS :]
    row = place_ref[1]
    side = lax.rem(row, 2)
    y = y_ref[...].T
    u = [u_ref[i].T for i in range(2)]
    left = split(rows(y, q_ref[...]))
    yu_split = split(lanes(y, *u))
    for d in range(LAYERS):
        ks = places(place_ref, d)
        low = [lanes(t_mine[d][i], t_other[d][i]) for i in range(2)]
        low += [lanes(l2_ref[ks[0], i], l2_ref[ks[1], i]) for i in range(2)]
        x = dot3(left, split(l32_ref[d]))
        z = dot3(yu_split, split(rows(*low)))
        for i, k in enumerate(ks):
            at = slice(i * TB, (i + 1) * TB)
            sum_ref[k, :TB] = x[:TB, at]
            sum_ref[k, TB : 2 * TB] = z[:, at]
            sum_ref[k, 2 * TB :] = x[TB:, at]
    for i in range(2):
        sum_ref[row - side + i, :TB] += u[i]


def finish_kernel(
    mask_ref, place_ref, f_ref, got_ref, home_ref, away_ref, q_home_ref, q_away_ref, out_ref
):
    even = lax.rem(place_ref[1], 2) == 0

    def masked(s, r, x):
        return jnp.where(mask_ref[s, r] == 1, x, 0.0)

    def both(home, away):
        return [jnp.where(even, home, away), jnp.where(even, away, home)]

    empty = jnp.zeros((TB, TB), F32)
    for r, c in ((0, 1), (0, 2), (0, 3), (1, 0), (1, 2), (1, 3), (2, 3)):
        out_ref[tile(r, c), :] = empty
    y = both(home_ref[...], away_ref[...])
    q = rows(*both(q_home_ref[...], q_away_ref[...]))
    q = jnp.where(even, q[:, :TB], q[:, TB:]).T
    parts = []
    for s in range(2):
        total = got_ref[s]
        for k in range(s + 2, N, 2):
            total += got_ref[k]
        out_ref[tile(s, s), :] = f_ref[tile(s, s), :] + total[TB : 2 * TB].T
        out_ref[tile(2, s), :] = masked(s, 2, -total[:TB].T)
        out_ref[tile(3, s), :] = masked(s, 3, y[s])
        parts.append(total[2 * TB :])
    out_ref[tile(2, 2), :] = f_ref[tile(2, 2), :] + rows(*parts).T
    out_ref[tile(3, 2), :] = masked(2, 3, -q)
    out_ref[tile(3, 3), :] = f_ref[tile(3, 3), :]


def swap_cores(x):
    return lax.ppermute(x, "col", CORE_SWAP)


def gather_layers(x, begin, ties):
    mine = {0: x}
    other = {}
    late = [0]
    up = down = x
    tied = []
    last = LAYERS // 2
    half = TB // 2
    beside = None
    for step in range(1, last + 1):
        swapped = [swap_cores(mine[d]) for d in late]
        if step == begin[0]:
            swapped, operand = lax.optimization_barrier((swapped, begin[1]))
            beside = begin[2](operand)
        if step == last:
            up, down = up[:, :half], down[:, half:]
        up = lax.ppermute(up, "col", LAYER_UP)
        down = lax.ppermute(down, "col", LAYER_DOWN)
        up, down, swapped, more = lax.optimization_barrier((up, down, swapped, ties.get(step)))
        tied.append(more)
        if step == begin[3]:
            up, down, beside = lax.optimization_barrier((up, down, beside))
        other.update(zip(late, swapped))
        if step < last:
            mine[LAYERS - step], mine[step] = up, down
            late = [LAYERS - step, step]
    mine[last] = jnp.concatenate([up, down], axis=1)
    other[last], beside = lax.optimization_barrier((swap_cores(mine[last]), beside))
    order = range(LAYERS)
    return [mine[d] for d in order], [other[d] for d in order], beside, *(t for t in tied if t is not None)


def body(factor, structure):
    row = lax.axis_index("row")
    col = lax.axis_index("col")
    place = jnp.stack([col, row]).astype(jnp.int32)
    mask = structure.reshape(4, 4, N)
    mask = lax.dynamic_index_in_dim(mask, row, axis=2, keepdims=False)
    flat = factor.reshape(N * TB, TB)
    square = (TB, TB)

    def to_rows(x):
        return lax.all_to_all(x, "row", 0, 0, tiled=True)

    def to_side(x):
        return lax.all_to_all(x, "row", 0, 0, tiled=True, axis_index_groups=SAME_SIDE)

    with jax.named_scope("prepare"):
        l32, away, home, send = call(
            prepare_kernel,
            [square, (4, *square), (4, *square), (N, TB + HALF, TB)],
            mask,
            place,
            flat,
            scalars=2,
        )
    with jax.named_scope("swap_l32"):
        l32_away = lax.ppermute(l32, "row", ROW_SWAP)
        even = lax.rem(row, 2) == 0
        l32_pair = jnp.stack([jnp.where(even, l32, l32_away), jnp.where(even, l32_away, l32)])
    with jax.named_scope("swap_rest"):
        l32_pair, away = lax.optimization_barrier((l32_pair, away))
        away = lax.ppermute(away, "row", ROW_SWAP)
    with jax.named_scope("gather_l"):
        l_mine, l_other, cols, away = gather_layers(
            l32_pair, (1, (send, away), lambda x: to_rows(x[0]), 4), {2: away}
        )
    with jax.named_scope("pack"):
        packed, l3 = call(pack_kernel, [(3, 2, *square), (2, *square)], place, home, away)
    with jax.named_scope("gather_rows"):
        panels = lax.all_gather(packed, "col", axis=0)
        panels = [panels[:, i] for i in range(3)]
        root_rows, diag_rows, l2_rows = panels
    with jax.named_scope("term_t"):
        t, send, l32_rows = call(
            t_kernel,
            [(2, *square), (N // 2, 2, *square), (LAYERS, 2 * TB, 2 * TB)],
            place,
            *l_mine,
            *l_other,
            cols,
            l3,
        )
    with jax.named_scope("term_uq"):
        u, q = call(
            uq_kernel,
            [(2, *square), (HALF, 2 * TB)],
            root_rows,
            diag_rows,
            cols,
            scalars=0,
        )
    with jax.named_scope("gather_t"):
        t_mine, t_other, t_cols, (root_rows, l2_rows), (u, q) = gather_layers(
            t, (1, send, to_side, 5), {3: (root_rows, l2_rows), 4: (u, q)}
        )
    with jax.named_scope("term_y"):
        y, y_home, y_away = call(
            y_kernel, [(2 * TB, TB), square, square], place, root_rows, t_cols
        )
    with jax.named_scope("swap_yq"):
        y_away = lax.ppermute(y_away, "row", ROW_SWAP)
        q_away = lax.ppermute(q, "row", ROW_SWAP)
    with jax.named_scope("sums"):
        (sums,) = call(
            sums_kernel,
            [(N, 2 * TB + HALF, TB)],
            place,
            *t_mine,
            *t_other,
            l32_rows,
            y,
            u,
            q,
            l2_rows,
        )
    with jax.named_scope("scatter_sums"):
        sums, y_away, q_away = lax.optimization_barrier((sums, y_away, q_away))
        got = lax.all_to_all(sums, "row", 0, 0, tiled=True)
    with jax.named_scope("finish"):
        (out,) = call(
            finish_kernel,
            [(N * TB, TB)],
            mask,
            place,
            flat,
            got,
            y_home,
            y_away,
            q,
            q_away,
            scalars=2,
        )
        return out.reshape(factor.shape)


def solution(mesh):
    return jax.shard_map(
        body,
        mesh=mesh,
        in_specs=(P(None, "row", None, "col"), P()),
        out_specs=P(None, "row", None, "col"),
        check_vma=False,
    )
```

```python
import jax
import jax.numpy as jnp
from jax import lax
from jax.experimental import pallas as pl
from jax.experimental.pallas import tpu as pltpu
from jax.sharding import PartitionSpec as P

N = 16
LAYERS = 8
TB = 128
HALF = 64
F32 = jnp.float32
BF16 = jnp.bfloat16
CORE_SWAP = [(i, i ^ 1) for i in range(N)]
ROW_SWAP = [(i, i ^ 1) for i in range(N)]
SAME_SIDE = [[p + 2 * i for i in range(N // 2)] for p in range(2)]
LAYER_UP = [(i, (i + 2) % N) for i in range(N)]
LAYER_DOWN = [(i, (i - 2) % N) for i in range(N)]


def split(x):
    high = x.astype(BF16)
    return high, (x - high.astype(F32)).astype(BF16)


def dot3(a, b):
    a_high, a_low = a
    b_high, b_low = b

    def one(x, y):
        return jnp.dot(x, y, preferred_element_type=F32)

    return one(a_high, b_high) + (one(a_high, b_low) + one(a_low, b_high))


def lanes(*tiles):
    return jnp.concatenate(tiles, axis=1)


def rows(*tiles):
    return jnp.concatenate(tiles, axis=0)


def tile(r, c):
    return pl.ds(r * 4 * TB + c, TB, stride=4)


def call(kernel, shapes, *args, scalars=1):
    smem = pl.BlockSpec(memory_space=pltpu.SMEM)
    vmem = pl.BlockSpec(memory_space=pltpu.VMEM)
    return pl.pallas_call(
        kernel,
        out_shape=[jax.ShapeDtypeStruct(s, F32) for s in shapes],
        in_specs=[smem] * scalars + [vmem] * (len(args) - scalars),
        out_specs=[vmem] * len(shapes),
        compiler_params=pltpu.CompilerParams(vmem_limit_bytes=5 * 2**20),
    )(*args)


def prepare_kernel(mask_ref, place_ref, f_ref, l32_ref, away_ref, home_ref, send_ref):
    side = lax.rem(place_ref[1], 2)

    def lower(r, c):
        return jnp.where(mask_ref[c, r] == 1, f_ref[tile(r, c), :], 0.0)

    x = lower(3, 2)
    l32_ref[...] = x
    turned = x.T
    l2 = [lower(2, s) for s in range(2)]
    l3 = [lower(3, s) for s in range(2)]
    for k in range(N):
        send_ref[k, :TB] = l2[k % 2]
        send_ref[k, TB:] = turned[k % 2 * HALF : (k % 2 + 1) * HALF]
    root, diag = f_ref[tile(3, 3), :], f_ref[tile(2, 2), :]
    away_ref[0] = home_ref[0] = root
    away_ref[1] = home_ref[1] = diag
    even = side == 0
    home_ref[2] = jnp.where(even, l2[0], l2[1])
    away_ref[2] = jnp.where(even, l2[1], l2[0])
    home_ref[3] = jnp.where(even, l3[0], l3[1])
    away_ref[3] = jnp.where(even, l3[1], l3[0])


def pack_kernel(place_ref, home_ref, got_ref, packed_ref, l3_ref):
    side = lax.rem(place_ref[1], 2)
    for i in range(3):
        packed_ref[i, side] = home_ref[i]
        packed_ref[i, 1 - side] = got_ref[i]
    l3_ref[side] = home_ref[3]
    l3_ref[1 - side] = got_ref[3]


def places(place_ref, d):
    layer, core = place_ref[0] // 2, lax.rem(place_ref[0], 2)
    k = lax.rem(layer + d, LAYERS) * 2
    return k + core, k + 1 - core


def t_kernel(place_ref, *refs):
    mine, other = refs[:LAYERS], refs[LAYERS : 2 * LAYERS]
    l2_ref, l3_ref, t_ref, send_ref, all_ref = refs[2 * LAYERS :]
    total = jnp.zeros((2 * TB, TB), F32)
    for d in range(LAYERS):
        k0, k1 = places(place_ref, d)
        a = rows(*(lanes(mine[d][i], other[d][i]) for i in range(2)))
        all_ref[d] = a
        total += dot3(split(a), split(rows(l2_ref[k0, :TB], l2_ref[k1, :TB])))
    for i in range(2):
        x = total[i * TB : (i + 1) * TB] - l3_ref[i]
        t_ref[i] = x
        for k in range(N // 2):
            send_ref[k, i] = x


def pair_rows(rows_ref, k):
    return rows(*(lanes(rows_ref[k, j], rows_ref[k + 1, j]) for j in range(2)))


def dot3_turned(a, b):
    def one(x, y):
        return lax.dot_general(x, y, (((1,), (1,)), ((), ())), preferred_element_type=F32)

    return one(a[0], b[0]) + (one(a[0], b[1]) + one(a[1], b[0]))


def uq_kernel(root_ref, diag_ref, cols_ref, u_ref, q_ref):
    u = jnp.zeros((2 * TB, TB), F32)
    q = jnp.zeros((HALF, 2 * TB), F32)
    for k in range(0, N, 2):
        b = split(rows(cols_ref[k, :TB], cols_ref[k + 1, :TB]))
        u += dot3(split(pair_rows(diag_ref, k)), b)
        b = split(lanes(cols_ref[k, TB:], cols_ref[k + 1, TB:]))
        q += dot3_turned(b, split(pair_rows(root_ref, k)))
    for i in range(2):
        u_ref[i] = u[i * TB : (i + 1) * TB]
    q_ref[...] = q


def y_kernel(place_ref, root_ref, t_ref, y_ref, home_ref, away_ref):
    y = jnp.zeros((2 * TB, TB), F32)
    for k in range(0, N, 2):
        b = split(rows(t_ref[k // 2, 0], t_ref[k // 2, 1]))
        y += dot3(split(pair_rows(root_ref, k)), b)
    y_ref[...] = y
    even = lax.rem(place_ref[1], 2) == 0
    home_ref[...] = jnp.where(even, y[:TB], y[TB:])
    away_ref[...] = jnp.where(even, y[TB:], y[:TB])


def sums_kernel(place_ref, *refs):
    t_mine, t_other = refs[:LAYERS], refs[LAYERS : 2 * LAYERS]
    l32_ref, y_ref, u_ref, q_ref, l2_ref, sum_ref = refs[2 * LAYERS :]
    row = place_ref[1]
    side = lax.rem(row, 2)
    y = y_ref[...].T
    u = [u_ref[i].T for i in range(2)]
    left = split(rows(y, q_ref[...]))
    yu_split = split(lanes(y, *u))
    for d in range(LAYERS):
        ks = places(place_ref, d)
        low = [lanes(t_mine[d][i], t_other[d][i]) for i in range(2)]
        low += [lanes(l2_ref[ks[0], i], l2_ref[ks[1], i]) for i in range(2)]
        x = dot3(left, split(l32_ref[d]))
        z = dot3(yu_split, split(rows(*low)))
        for i, k in enumerate(ks):
            at = slice(i * TB, (i + 1) * TB)
            sum_ref[k, :TB] = x[:TB, at]
            sum_ref[k, TB : 2 * TB] = z[:, at]
            sum_ref[k, 2 * TB :] = x[TB:, at]
    for i in range(2):
        sum_ref[row - side + i, :TB] += u[i]


def finish_kernel(
    mask_ref, place_ref, f_ref, got_ref, home_ref, away_ref, q_home_ref, q_away_ref, out_ref
):
    even = lax.rem(place_ref[1], 2) == 0

    def masked(s, r, x):
        return jnp.where(mask_ref[s, r] == 1, x, 0.0)

    def both(home, away):
        return [jnp.where(even, home, away), jnp.where(even, away, home)]

    empty = jnp.zeros((TB, TB), F32)
    for r, c in ((0, 1), (0, 2), (0, 3), (1, 0), (1, 2), (1, 3), (2, 3)):
        out_ref[tile(r, c), :] = empty
    y = both(home_ref[...], away_ref[...])
    q = rows(*both(q_home_ref[...], q_away_ref[...]))
    q = jnp.where(even, q[:, :TB], q[:, TB:]).T
    parts = []
    for s in range(2):
        total = got_ref[s]
        for k in range(s + 2, N, 2):
            total += got_ref[k]
        out_ref[tile(s, s), :] = f_ref[tile(s, s), :] + total[TB : 2 * TB].T
        out_ref[tile(2, s), :] = masked(s, 2, -total[:TB].T)
        out_ref[tile(3, s), :] = masked(s, 3, y[s])
        parts.append(total[2 * TB :])
    out_ref[tile(2, 2), :] = f_ref[tile(2, 2), :] + rows(*parts).T
    out_ref[tile(3, 2), :] = masked(2, 3, -q)
    out_ref[tile(3, 3), :] = f_ref[tile(3, 3), :]


def swap_cores(x):
    return lax.ppermute(x, "col", CORE_SWAP)


def gather_layers(x, begin, ties):
    mine = {0: x}
    other = {}
    late = [0]
    up = down = x
    tied = []
    last = LAYERS // 2
    half = TB // 2
    beside = None
    for step in range(1, last + 1):
        swapped = [swap_cores(mine[d]) for d in late]
        if step == begin[0]:
            swapped, operand = lax.optimization_barrier((swapped, begin[1]))
            beside = begin[2](operand)
        if step == last:
            up, down = up[:, :half], down[:, half:]
        up = lax.ppermute(up, "col", LAYER_UP)
        down = lax.ppermute(down, "col", LAYER_DOWN)
        more = ties.get(step)
        if callable(more):
            more = more(tied[-1])
        up, down, swapped, more = lax.optimization_barrier((up, down, swapped, more))
        tied.append(more)
        if step == begin[3]:
            up, down, beside = lax.optimization_barrier((up, down, beside))
        other.update(zip(late, swapped))
        if step < last:
            mine[LAYERS - step], mine[step] = up, down
            late = [LAYERS - step, step]
    mine[last] = jnp.concatenate([up, down], axis=1)
    other[last], beside = lax.optimization_barrier((swap_cores(mine[last]), beside))
    order = range(LAYERS)
    return [mine[d] for d in order], [other[d] for d in order], beside, *(t for t in tied if t is not None)


def body(factor, structure):
    row = lax.axis_index("row")
    col = lax.axis_index("col")
    place = jnp.stack([col, row]).astype(jnp.int32)
    mask = structure.reshape(4, 4, N)
    mask = lax.dynamic_index_in_dim(mask, row, axis=2, keepdims=False)
    flat = factor.reshape(N * TB, TB)
    square = (TB, TB)

    def to_rows(x):
        return lax.all_to_all(x, "row", 0, 0, tiled=True)

    def to_side(x):
        return lax.all_to_all(x, "row", 0, 0, tiled=True, axis_index_groups=SAME_SIDE)

    with jax.named_scope("prepare"):
        l32, away, home, send = call(
            prepare_kernel,
            [square, (4, *square), (4, *square), (N, TB + HALF, TB)],
            mask,
            place,
            flat,
            scalars=2,
        )
    with jax.named_scope("swap_l32"):
        l32_away = lax.ppermute(l32, "row", ROW_SWAP)
        even = lax.rem(row, 2) == 0
        l32_pair = jnp.stack([jnp.where(even, l32, l32_away), jnp.where(even, l32_away, l32)])
    with jax.named_scope("swap_rest"):
        l32_pair, away = lax.optimization_barrier((l32_pair, away))
        away = lax.ppermute(away, "row", ROW_SWAP)
    def pack(away):
        return call(pack_kernel, [(3, 2, *square), (2, *square)], place, home, away)

    with jax.named_scope("gather_l"):
        l_mine, l_other, cols, _, (packed, l3) = gather_layers(
            l32_pair, (2, (send, away), lambda x: to_rows(x[0]), 4), {1: away, 2: pack}
        )
    with jax.named_scope("gather_rows"):
        panels = lax.all_gather(packed, "col", axis=0)
        panels = [panels[:, i] for i in range(3)]
        root_rows, diag_rows, l2_rows = panels
    with jax.named_scope("term_t"):
        t, send, l32_rows = call(
            t_kernel,
            [(2, *square), (N // 2, 2, *square), (LAYERS, 2 * TB, 2 * TB)],
            place,
            *l_mine,
            *l_other,
            cols,
            l3,
        )
    with jax.named_scope("term_uq"):
        u, q = call(
            uq_kernel,
            [(2, *square), (HALF, 2 * TB)],
            root_rows,
            diag_rows,
            cols,
            scalars=0,
        )
    with jax.named_scope("gather_t"):
        t_mine, t_other, t_cols, (root_rows, l2_rows), (u, q) = gather_layers(
            t, (1, send, to_side, 5), {3: (root_rows, l2_rows), 4: (u, q)}
        )
    with jax.named_scope("term_y"):
        y, y_home, y_away = call(
            y_kernel, [(2 * TB, TB), square, square], place, root_rows, t_cols
        )
    with jax.named_scope("swap_yq"):
        y_away = lax.ppermute(y_away, "row", ROW_SWAP)
        q_away = lax.ppermute(q, "row", ROW_SWAP)
    with jax.named_scope("sums"):
        (sums,) = call(
            sums_kernel,
            [(N, 2 * TB + HALF, TB)],
            place,
            *t_mine,
            *t_other,
            l32_rows,
            y,
            u,
            q,
            l2_rows,
        )
    with jax.named_scope("scatter_sums"):
        sums, y_away, q_away = lax.optimization_barrier((sums, y_away, q_away))
        got = lax.all_to_all(sums, "row", 0, 0, tiled=True)
    with jax.named_scope("finish"):
        (out,) = call(
            finish_kernel,
            [(N * TB, TB)],
            mask,
            place,
            flat,
            got,
            y_home,
            y_away,
            q,
            q_away,
            scalars=2,
        )
        return out.reshape(factor.shape)


def solution(mesh):
    return jax.shard_map(
        body,
        mesh=mesh,
        in_specs=(P(None, "row", None, "col"), P()),
        out_specs=P(None, "row", None, "col"),
        check_vma=False,
    )
```
